32 devices in a mesh: fsdp: 2 (over x), context: 4 (over y, core), tensor: 4 (over z).
Axes of the slice: x: 2, y: 2, z: 4, core: 2. Of those that a mesh axis runs over, the one named last changes fastest.
Arguments:
- hidden_in: bfloat16 [4096, 2048], P(('fsdp', 'context')), may hold values from -6 to 6
- segments: int32 [2, 2048], P('fsdp'), may hold values from 0 to 4, as said below
- cotangent: bfloat16 [4096, 2048], P(('fsdp', 'context')), may hold values from -6 to 6
- attn_gain: bfloat16 [2048], P(('fsdp', 'context')), may hold values from 0.25 to 1.75
- query_weight: bfloat16 [2048, 2048], P(('fsdp', 'context'), 'tensor'), may hold values from -0.125 to 0.125
- key_weight: bfloat16 [2048, 1024], P(('fsdp', 'context'), 'tensor'), may hold values from -0.125 to 0.125
- value_weight: bfloat16 [2048, 1024], P(('fsdp', 'context'), 'tensor'), may hold values from -0.125 to 0.125
- output_weight: bfloat16 [2048, 2048], P(('fsdp', 'context'), 'tensor'), may hold values from -3 to 3
- qnorm_gain: bfloat16 [128], replicated, may hold values from 0.25 to 1.75
- knorm_gain: bfloat16 [128], replicated, may hold values from 0.25 to 1.75
- ffn_gain: bfloat16 [2048], P(('fsdp', 'context')), may hold values from 0.25 to 1.75
- gate_weight: bfloat16 [2048, 6144], P(('fsdp', 'context'), 'tensor'), may hold values from -0.125 to 0.125
- up_weight: bfloat16 [2048, 6144], P(('fsdp', 'context'), 'tensor'), may hold values from -0.125 to 0.125
- down_weight: bfloat16 [2048, 6144], P(('fsdp', 'context'), 'tensor'), may hold values from -0.109375 to 0.109375
Outputs:
- output: bfloat16 [4096, 2048], P(('fsdp', 'context'))
- input_grad: float32 [4096, 2048], P(('fsdp', 'context'))
- attn_gain_grad: float32 [2048], P(('fsdp', 'context'))
- query_grad: float32 [2048, 2048], P(('fsdp', 'context'), 'tensor')
- key_grad: float32 [2048, 1024], P(('fsdp', 'context'), 'tensor')
- value_grad: float32 [2048, 1024], P(('fsdp', 'context'), 'tensor')
- output_grad: float32 [2048, 2048], P(('fsdp', 'context'), 'tensor')
- qnorm_grad: float32 [128], replicated
- knorm_grad: float32 [128], replicated
- ffn_gain_grad: float32 [2048], P(('fsdp', 'context'))
- gate_grad: float32 [2048, 6144], P(('fsdp', 'context'), 'tensor')
- up_grad: float32 [2048, 6144], P(('fsdp', 'context'), 'tensor')
- down_grad: float32 [2048, 6144], P(('fsdp', 'context'), 'tensor')
The draws below stay inside these ranges and needn't reach their ends.
Inputs may be any that keep to these rules, and one draw needn't show every extreme that they name: `segments`: document numbers never fall along the positions of a sequence; in every sequence one document covers positions 255 to 1792; the first position has number 0 and the last number 4; some numbers may be skipped.
All inputs are finite; a program needn't handle non-finite values.
Results may differ from the reference program's by a relative error of at most 0.014.
Values may be sent and summed in bfloat16 or wider, within the bound.
No kernel may reach another device: no remote copies, remote signals or barrier semaphores. Data moves between devices by JAX's collectives and lax.ppermute only.
A program may use at most 256 MiB of HBM per device.

```python
import jax
import jax.numpy as jnp
from jax import lax

D = 2048
HEADS = 16
KV_HEADS = 8
HEAD_DIM = 128
FF = 6144
TOK_DEV = 512
SEQ = 2048
SEQS = 2
TOKENS = 4096
N_CONTEXT = 4


def draw_segments(key, part):
    key = jax.random.fold_in(key, 7)
    key_start, key_stop, key_early, key_late = jax.random.split(key, 4)
    half_rows = TOK_DEV // 2
    long_start = jax.random.randint(key_start, (SEQS, 1), 1, half_rows)
    long_stop = jax.random.randint(key_stop, (SEQS, 1), SEQ - half_rows + 1, SEQ)
    early_cut = jax.random.randint(key_early, (SEQS, 1), 1, long_start + 1)
    late_cut = jax.random.randint(key_late, (SEQS, 1), long_stop, SEQ)
    position = jnp.arange(SEQ, dtype=jnp.int32)[None, :]
    return (position >= early_cut).astype(jnp.int32) + (position >= long_start).astype(jnp.int32) + (position >= long_stop).astype(jnp.int32) + (position >= late_cut).astype(jnp.int32)


def block_levels(rng, shape, cuts, least, top_value):
    def one(axis_at, parts):
        draws = jax.random.uniform(jax.random.fold_in(jax.random.fold_in(rng, 6), axis_at), (parts,), jnp.float32, least / len(cuts), top_value / len(cuts))
        return jnp.repeat(jnp.exp(draws), shape[axis_at] // parts).reshape((-1,) + (1,) * (len(shape) - axis_at - 1))

    level = one(*cuts[0])
    for cut in cuts[1:]:
        level = level * one(*cut)
    return level


def bell_draw(key, shape, width, limit, shards=(), kind=jnp.bfloat16):
    gain = block_levels(key, shape, shards, -0.22, 0.18) if shards else 1.0
    values = jax.random.normal(key, shape, jnp.float32) * width * gain
    return jnp.minimum(jnp.maximum(values, -limit), limit).astype(kind)


def setup_inputs(seed: int = 0) -> dict:
    key_of = jax.random.split(jax.random.key(seed), 15)
    return {
        "hidden_in": bell_draw(key_of[0], (TOKENS, D), 1.0, 6.0, ((0, 8),)),
        "segments": draw_segments(jax.random.fold_in(key_of[14], 71), 0),
        "cotangent": bell_draw(key_of[2], (TOKENS, D), 1.0, 6.0, ((0, 8),)),
        "attn_gain": jnp.clip(1.0 + 0.15 * jax.random.normal(key_of[3], (D,), jnp.float32), 0.25, 1.75).astype(jnp.bfloat16),
        "query_weight": bell_draw(key_of[4], (D, HEADS * HEAD_DIM), D ** -0.5, 0.125, ((0, 8), (1, 4))),
        "key_weight": bell_draw(key_of[5], (D, KV_HEADS * HEAD_DIM), D ** -0.5, 0.125, ((0, 8), (1, 4))),
        "value_weight": bell_draw(key_of[6], (D, KV_HEADS * HEAD_DIM), D ** -0.5, 0.125, ((0, 8), (1, 4))),
        "output_weight": bell_draw(key_of[7], (D, HEADS * HEAD_DIM), 4 ** -0.5, 3.0, ((0, 8), (1, 4))),
        "qnorm_gain": jnp.clip(1.0 + 0.15 * jax.random.normal(key_of[8], (HEAD_DIM,), jnp.float32), 0.25, 1.75).astype(jnp.bfloat16),
        "knorm_gain": jnp.clip(1.0 + 0.15 * jax.random.normal(key_of[9], (HEAD_DIM,), jnp.float32), 0.25, 1.75).astype(jnp.bfloat16),
        "ffn_gain": jnp.clip(1.0 + 0.15 * jax.random.normal(key_of[10], (D,), jnp.float32), 0.25, 1.75).astype(jnp.bfloat16),
        "gate_weight": bell_draw(key_of[11], (D, FF), D ** -0.5, 0.125, ((0, 8), (1, 4))),
        "up_weight": bell_draw(key_of[12], (D, FF), D ** -0.5, 0.125, ((0, 8), (1, 4))),
        "down_weight": bell_draw(key_of[13], (D, FF), (FF // 2) ** -0.5, 0.109375, ((0, 8), (1, 4))),
    }


EPS = 1e-06
THETA = 1000000.0

@jax.custom_vjp
def low(v):
    return lax.optimization_barrier(v.astype(jnp.bfloat16)).astype(jnp.float32)

@jax.custom_vjp
def low_back(v):
    return v

def low_keep(v):
    return (low(v), None)

def low_pass(kept, grad):
    return (grad,)

def back_keep(v):
    return (v, None)

def back_low(kept, grad):
    return (low(grad),)
low.defvjp(low_keep, low_pass)
low_back.defvjp(back_keep, back_low)

def matmul(matrix_a, matrix_b):
    return jnp.dot(matrix_a, matrix_b, precision=lax.Precision.HIGHEST, preferred_element_type=jnp.float32)

def rms_scale(values):
    return lax.rsqrt(lax.optimization_barrier(jnp.mean(values * values, axis=-1, keepdims=True)) + EPS)

def stored_positions(length, pieces):
    half_rows = length // (2 * pieces)
    rows = jnp.arange(length, dtype=jnp.int32)
    block = rows // half_rows
    owner = block // 2
    place = jnp.where(block % 2 == 0, owner, 2 * pieces - 1 - owner)
    return (place * half_rows + rows % half_rows).astype(jnp.int32)

def rotary(values, positions):
    half_dim = values.shape[-1] // 2
    inverse = THETA ** (-(jnp.arange(half_dim).astype(jnp.float32) * 2.0 / values.shape[-1]))
    angles = positions.astype(jnp.float32)[:, None] * inverse[None, :]
    cosine = jnp.cos(angles)[:, None, :]
    sine_table = jnp.sin(angles)[:, None, :]
    first_half = values[..., :half_dim]
    second_half = values[..., half_dim:]
    return jnp.concatenate([first_half * cosine - second_half * sine_table, second_half * cosine + first_half * sine_table], axis=-1)

def forward(hidden, positions, seg_row, attn_gain, query_weight, key_weight, value_weight, output_weight, qnorm_gain, knorm_gain, ffn_gain, gate_weight, up_weight, down_weight):
    length = hidden.shape[0]
    group_size = HEADS // KV_HEADS
    normed_one = low(hidden * rms_scale(hidden) * attn_gain)
    query_proj = low_back(matmul(normed_one, query_weight)).reshape(length, HEADS, HEAD_DIM)
    key_proj = low_back(matmul(normed_one, key_weight)).reshape(length, KV_HEADS, HEAD_DIM)
    value_proj = low_back(low(matmul(normed_one, value_weight))).reshape(length, KV_HEADS, HEAD_DIM)
    queries = low_back(low(rotary(query_proj * rms_scale(query_proj) * qnorm_gain, positions)))
    keys = low_back(low(rotary(key_proj * rms_scale(key_proj) * knorm_gain, positions)))
    block_rows = 512 if length % 512 == 0 else length
    factor = HEAD_DIM ** (-0.5)
    query_blocks = queries.reshape(length // block_rows, block_rows, KV_HEADS, group_size, HEAD_DIM)

    def attend(operands):
        query_block, pos_block, seg_block = operands
        scores = low_back(jnp.einsum('bkgd,skd->bkgs', query_block, keys, precision=lax.Precision.HIGHEST) * factor)
        allowed = (positions[None, :] <= pos_block[:, None]) & (seg_row[None, :] == seg_block[:, None])
        scores = jnp.where(allowed[:, None, None, :], scores, -1e+30)
        row_top = lax.optimization_barrier(jnp.max(scores, axis=-1, keepdims=True))
        exponent = jnp.exp(scores - row_top)
        probability = low(exponent / lax.optimization_barrier(jnp.sum(exponent, axis=-1, keepdims=True)))
        return jnp.einsum('bkgs,skd->bkgd', probability, value_proj, precision=lax.Precision.HIGHEST)
    attended = lax.map(jax.checkpoint(attend), (query_blocks, positions.reshape(-1, block_rows), seg_row.reshape(-1, block_rows)))
    attended = low_back(low(attended.reshape(length, HEADS * HEAD_DIM)))
    middle = hidden + low_back(matmul(attended, output_weight.T))
    normed_two = low(middle * rms_scale(middle) * ffn_gain)
    gate_in = low_back(matmul(normed_two, gate_weight))
    up_in = low_back(matmul(normed_two, up_weight))
    product = low(jax.nn.silu(gate_in) * up_in)
    return middle + low_back(matmul(product, down_weight.T))

def reference(hidden_in, segments, cotangent, attn_gain, query_weight, key_weight, value_weight, output_weight, qnorm_gain, knorm_gain, ffn_gain, gate_weight, up_weight, down_weight):
    weights = tuple((item.astype(jnp.float32) for item in (attn_gain, query_weight, key_weight, value_weight, output_weight, qnorm_gain, knorm_gain, ffn_gain, gate_weight, up_weight, down_weight)))
    rows_in = hidden_in.astype(jnp.float32).reshape(SEQS, SEQ, D)
    cot_rows = cotangent.astype(jnp.float32).reshape(SEQS, SEQ, D)
    positions = stored_positions(SEQ, N_CONTEXT)

    def one_sequence(totals, operands):
        hidden, seg_pos, cot_row = operands
        seg_row = jnp.take(seg_pos, positions)

        def layer_fn(hidden_arg, *params):
            return forward(hidden_arg, positions, seg_row, *params)
        result, pullback = jax.vjp(layer_fn, hidden, *weights)
        gradients = pullback(cot_row)
        summed = tuple((running + update for running, update in zip(totals, gradients[1:])))
        return (summed, (result.astype(jnp.bfloat16), gradients[0]))
    zero_init = tuple((jnp.zeros(item.shape, jnp.float32) for item in weights))
    totals, (outputs, input_grads) = lax.scan(one_sequence, zero_init, (rows_in, segments, cot_rows))
    return (outputs.reshape(TOKENS, D), input_grads.reshape(TOKENS, D), totals[0], totals[1], totals[2], totals[3], totals[4], totals[5], totals[6], totals[7], totals[8], totals[9], totals[10])
```

```python
import functools

import jax
import jax.numpy as jnp
from jax import lax
from jax.experimental import pallas as pl
from jax.experimental.pallas import tpu as pltpu
from jax.sharding import PartitionSpec as P

EPS = 1e-06
THETA = 1000000.0
ROWS = ("fsdp", "context")
LOW = jnp.bfloat16
F32 = jnp.float32
LOG2E = 1.4426950408889634
VMEM_BYTES = 56 * 1024 * 1024


def dot_plain(matrix_a, matrix_b):
    return jnp.dot(matrix_a, matrix_b, preferred_element_type=F32)


def dot_right_t(matrix_a, matrix_b):
    return lax.dot_general(matrix_a, matrix_b, (((1,), (1,)), ((), ())), preferred_element_type=F32)


def dot_left_t(matrix_a, matrix_b):
    return lax.dot_general(matrix_a, matrix_b, (((0,), (0,)), ((), ())), preferred_element_type=F32)


def tie(*items):
    return lax.optimization_barrier(items)


def rms_scale(values):
    return lax.rsqrt(jnp.mean(values * values, axis=-1, keepdims=True) + EPS)


def gather_rows(shard):
    return lax.all_gather(shard, ROWS, axis=0, tiled=True)


def scatter_rows(full):
    return lax.psum_scatter(full.astype(LOW), ROWS, scatter_dimension=0, tiled=True)


def sum_tensor(partial):
    return lax.psum(partial.astype(LOW), "tensor")


def add_low(mine, other):
    return (mine.astype(F32) + other.astype(F32)).astype(LOW)


def place(index):
    return index // 4, (index // 2) % 2, index % 2


def staged_pairs(step):
    pairs = []
    for index in range(8):
        x, y, core = place(index)
        if step == "core":
            core = 1 - core
        elif (step == "first") == (core == 0):
            x = 1 - x
        else:
            y = 1 - y
        pairs.append((index, x * 4 + y * 2 + core))
    return pairs


def staged(values, step):
    return lax.ppermute(values, ROWS, staged_pairs(step))


def staged_blocks():
    x, y, core = place(lax.axis_index(ROWS))
    blocks = []
    for step in range(8):
        d_core, d_second, d_first = step // 4, (step // 2) % 2, step % 2
        its_core = core ^ d_core
        its_x = x ^ jnp.where(its_core == 0, d_first, d_second)
        its_y = y ^ jnp.where(its_core == 0, d_second, d_first)
        blocks.append(its_x * 4 + its_y * 2 + its_core)
    return jnp.stack(blocks).astype(jnp.int32)


def staged_gather(shard):
    pair = jnp.concatenate([shard, staged(shard, "first")])
    quad = jnp.concatenate([pair, staged(pair, "second")])
    return jnp.concatenate([quad, staged(quad, "core")])


def staged_scatter(full):
    rows = full.shape[0] // 8
    quad = add_low(full[: 4 * rows], staged(full[4 * rows :], "core"))
    pair = add_low(quad[: 2 * rows], staged(quad[2 * rows :], "second"))
    return pair[:rows].astype(F32) + staged(pair[rows:], "first").astype(F32)


def swap_context(values, bit):
    size = lax.axis_size("context")
    return lax.ppermute(values, "context", [(index, index ^ bit) for index in range(size)])


def params():
    return pltpu.CompilerParams(vmem_limit_bytes=VMEM_BYTES)


def cost(flops, moved):
    return pl.CostEstimate(flops=int(flops), bytes_accessed=int(moved), transcendentals=0)


def whole(shape):
    return pl.BlockSpec(shape, lambda *_: (0,) * len(shape))


def column(ids, step, width):
    return pl.ds(pl.multiple_of(ids[step] * width, width), width)


def first_norm_kernel(ids, hidden, gain, staged_out):
    width = gain.shape[1]
    scale = rms_scale(hidden[...].astype(F32))
    for step in range(gain.shape[0]):
        part = hidden[:, column(ids, step, width)].astype(F32) * scale * gain[step : step + 1, :]
        staged_out[:, step * width : (step + 1) * width] = part.astype(LOW)


def second_norm_kernel(ids, hidden, attn, gain, middle, plain_out, staged_out):
    width = gain.shape[1]
    for step in range(gain.shape[0]):
        spot = column(ids, step, width)
        middle[:, spot] = hidden[:, spot].astype(F32) + attn[:, step * width : (step + 1) * width].astype(F32)
    scale = rms_scale(middle[...])
    for step in range(gain.shape[0]):
        spot = column(ids, step, width)
        part = (middle[:, spot] * scale * gain[step : step + 1, :]).astype(LOW)
        plain_out[:, spot] = part
        staged_out[:, step * width : (step + 1) * width] = part


def second_back_kernel(ids, grad, middle, cotangent, gain, dmiddle, staged_out):
    width = gain.shape[1]
    scale = rms_scale(middle[...])
    total = jnp.zeros_like(scale)
    for step in range(gain.shape[0]):
        spot = column(ids, step, width)
        part = grad[:, spot].astype(F32) * gain[step : step + 1, :] * middle[:, spot]
        total = total + jnp.sum(part, axis=-1, keepdims=True)
    mean = total * scale / middle.shape[1]
    for step in range(gain.shape[0]):
        spot = column(ids, step, width)
        part = grad[:, spot].astype(F32) * gain[step : step + 1, :] - middle[:, spot] * (scale * mean)
        part = cotangent[:, spot].astype(F32) + scale * part
        dmiddle[:, spot] = part
        staged_out[:, step * width : (step + 1) * width] = part.astype(LOW)


def first_back_kernel(ids, grad, hidden, dmiddle, gain, out):
    width = gain.shape[1]
    scale = rms_scale(hidden[...].astype(F32))
    total = jnp.zeros_like(scale)
    for step in range(gain.shape[0]):
        spot = column(ids, step, width)
        part = grad[:, step * width : (step + 1) * width].astype(F32) * gain[step : step + 1, :]
        total = total + jnp.sum(part * hidden[:, spot].astype(F32), axis=-1, keepdims=True)
    mean = total * scale / hidden.shape[1]
    for step in range(gain.shape[0]):
        spot = column(ids, step, width)
        part = grad[:, step * width : (step + 1) * width].astype(F32) * gain[step : step + 1, :]
        out[:, spot] = dmiddle[:, spot] + scale * (part - hidden[:, spot].astype(F32) * (scale * mean))


def row_call(kernel, ids, arrays, gain, out_types):
    rows, width = arrays[0].shape
    tile = min(128, rows)
    spec = pl.BlockSpec((tile, width), lambda step, *_: (step, 0))
    moved = sum(item.size * item.dtype.itemsize for item in arrays) + sum(
        rows * width * jnp.dtype(kind).itemsize for kind in out_types
    )
    return pl.pallas_call(
        kernel,
        grid_spec=pltpu.PrefetchScalarGridSpec(
            num_scalar_prefetch=1,
            grid=(rows // tile,),
            in_specs=[spec] * len(arrays) + [whole(gain.shape)],
            out_specs=[spec] * len(out_types),
        ),
        out_shape=[jax.ShapeDtypeStruct((rows, width), kind) for kind in out_types],
        compiler_params=params(),
        cost_estimate=cost(10 * rows * width, moved),
    )(ids, *arrays, gain)


def rotate(values, cosine, sine):
    return values * cosine + pltpu.roll(values, values.shape[1] // 2, 1) * sine


def head_forward(proj, gain, cosine, sine):
    scale = rms_scale(proj)
    unit = proj * scale
    return rotate(unit * gain, cosine, sine).astype(LOW), unit, scale


def head_backward(grad, unit, scale, gain, cosine, sine):
    turned = rotate(grad.astype(LOW).astype(F32), cosine, -sine)
    scaled = turned * gain
    back = scale * (scaled - unit * jnp.mean(scaled * unit, axis=-1, keepdims=True))
    rows, width = grad.shape
    return back.astype(LOW), jnp.sum((turned * unit).reshape(rows // 8, 8, width), axis=0)


def key_forward_kernel(proj, gain, cosine, sine, out):
    dim = gain.shape[1]
    for head in range(proj.shape[1] // (2 * dim)):
        at = 2 * head * dim
        out[:, at : at + dim] = head_forward(proj[:, at : at + dim], gain[...], cosine[...], sine[...])[0]
        out[:, at + dim : at + 2 * dim] = proj[:, at + dim : at + 2 * dim].astype(LOW)


def key_backward_kernel(mine, other, proj, gain, cosine, sine, out, norm_out):
    dim = gain.shape[1]
    total = jnp.zeros(norm_out.shape, F32)
    for head in range(proj.shape[1] // (2 * dim)):
        at = 2 * head * dim
        scale = rms_scale(proj[:, at : at + dim])
        unit = proj[:, at : at + dim] * scale
        grad = mine[:, at : at + dim].astype(F32) + other[:, at : at + dim].astype(F32)
        back, norm = head_backward(grad, unit, scale, gain[...], cosine[...], sine[...])
        total = total + norm
        out[:, at : at + dim] = back
        spot = slice(at + dim, at + 2 * dim)
        out[:, spot] = (mine[:, spot].astype(F32) + other[:, spot].astype(F32)).astype(LOW)
    norm_out[...] = total


def pair_of(info, step):
    first = info[0]
    late = step > first
    piece = jnp.where(late, 1, 0)
    key_block = jnp.where(late, step - first - 1, step)
    query_block = jnp.where(late, info[1], first)
    return piece, key_block, query_block, info[2 + key_block]


def allowed_pair(shape, half, query_block, key_block, query_seg, key_seg):
    row = lax.rem(lax.broadcasted_iota(jnp.int32, shape, 0), half)
    col = lax.broadcasted_iota(jnp.int32, shape, 1)
    return (col - row <= (query_block - key_block) * half) & (query_seg == key_seg)


def attend_kernel(half, info, qproj, kv, gain, cosine, sine, seg_row, seg_col, out, out_wide, log_out, qs, acc, total, segq):
    dim = gain.shape[1]
    group = qproj.shape[1] // dim
    pairs = info.shape[0] - 1
    factor = LOG2E * dim ** (-0.5)
    for head in range(group):
        cols = slice(head * dim, (head + 1) * dim)
        query = head_forward(qproj[:, cols], gain[...], cosine[...], sine[...])[0]
        for piece in range(2):
            spot = slice(head * half, (head + 1) * half)
            rows = slice(piece * half, (piece + 1) * half)
            qs[piece, spot, :] = query[rows]
            segq[piece, spot, :] = seg_col[rows, :]
    acc[...] = jnp.zeros_like(acc)
    total[...] = jnp.zeros_like(total)
    for step in range(pairs):
        piece, key_block, query_block, spot = pair_of(info, step)
        rows = pl.ds(pl.multiple_of(spot * half, half), half)
        scores = dot_right_t(qs[piece], kv[rows, :dim])
        key_seg = seg_row[:, pl.ds(pl.multiple_of(key_block * half, half), half)]
        allowed = allowed_pair(scores.shape, half, query_block, key_block, segq[piece], key_seg)
        weight = jnp.where(allowed, jnp.exp2(scores * factor), 0.0)
        total[piece] += sum(weight[:, at : at + 128] for at in range(0, half, 128))
        acc[piece] += dot_plain(weight.astype(LOW), kv[rows, dim:])
    for piece in range(2):
        sums = jnp.sum(total[piece], axis=-1, keepdims=True)
        result = acc[piece] / sums
        logs = jnp.broadcast_to(jnp.log2(sums), result.shape)
        for head in range(group):
            cols = slice(head * dim, (head + 1) * dim)
            rows = slice(piece * half, (piece + 1) * half)
            part = result[head * half : (head + 1) * half]
            out[rows, cols] = part.astype(LOW)
            out_wide[rows, cols] = part
            log_out[rows, cols] = logs[head * half : (head + 1) * half]


def attend_back_kernel(
    half, info, qproj, kv, wide, logs, grad, gain, cosine, sine, seg_row, seg_col,
    dq_out, dkv_out, norm_out, qs, gs, segq, ls, ds, dq, dkv,
):
    dim = gain.shape[1]
    group = qproj.shape[1] // dim
    pairs = info.shape[0] - 1
    plain = dim ** (-0.5)
    factor = LOG2E * plain
    for head in range(group):
        cols = slice(head * dim, (head + 1) * dim)
        query = head_forward(qproj[:, cols], gain[...], cosine[...], sine[...])[0]
        delta = jnp.sum(grad[:, cols].astype(F32) * wide[:, cols], axis=-1, keepdims=True)
        for piece in range(2):
            spot = slice(head * half, (head + 1) * half)
            rows = slice(piece * half, (piece + 1) * half)
            qs[piece, spot, :] = query[rows]
            gs[piece, spot, :] = grad[rows, cols]
            segq[piece, spot, :] = seg_col[rows, :]
            ls[piece, spot, :] = logs[rows, head * dim : head * dim + 1]
            ds[piece, spot, :] = delta[rows]
    dq[...] = jnp.zeros_like(dq)
    dkv[...] = jnp.zeros_like(dkv)
    for step in range(pairs):
        piece, key_block, query_block, spot = pair_of(info, step)
        rows = pl.ds(pl.multiple_of(spot * half, half), half)
        query, outer = qs[piece], gs[piece]
        scores = dot_right_t(query, kv[rows, :dim])
        key_seg = seg_row[:, pl.ds(pl.multiple_of(key_block * half, half), half)]
        allowed = allowed_pair(scores.shape, half, query_block, key_block, segq[piece], key_seg)
        prob = jnp.where(allowed, jnp.exp2(scores * factor - ls[piece]), 0.0)
        dprob = dot_right_t(outer, kv[rows, dim:])
        dscores = (prob * (dprob - ds[piece])).astype(LOW)
        dq[piece] += dot_plain(dscores, kv[rows, :dim])
        dkv[rows, :dim] += dot_left_t(dscores, query)
        dkv[rows, dim:] += dot_left_t(prob.astype(LOW), outer)
    dkv_out[:, :dim] = (dkv[:, :dim] * plain).astype(LOW)
    dkv_out[:, dim:] = dkv[:, dim:].astype(LOW)
    total = jnp.zeros(norm_out.shape[1:], F32)
    for head in range(group):
        cols = slice(head * dim, (head + 1) * dim)
        scale = rms_scale(qproj[:, cols])
        unit = qproj[:, cols] * scale
        grads = jnp.concatenate([dq[piece, head * half : (head + 1) * half, :] for piece in range(2)]) * plain
        back, norm = head_backward(grads, unit, scale, gain[...], cosine[...], sine[...])
        total = total + norm
        dq_out[:, cols] = back
    norm_out[0] = total


def heads_spec(rows, width):
    return pl.BlockSpec((rows, width), lambda head, *_: (0, head))


def attend(info, qproj, kv, gain, cosine, sine, seg_row, seg_col):
    rows, qcols = qproj.shape
    total_rows, kvcols = kv.shape
    dim = gain.shape[1]
    heads = kvcols // (2 * dim)
    wide = qcols // heads
    half = rows // 2
    stacked = half * (wide // dim)
    qspec, kspec = heads_spec(rows, wide), heads_spec(total_rows, 2 * dim)
    return pl.pallas_call(
        functools.partial(attend_kernel, half),
        grid_spec=pltpu.PrefetchScalarGridSpec(
            num_scalar_prefetch=1,
            grid=(heads,),
            in_specs=[qspec, kspec, whole(gain.shape), whole(cosine.shape), whole(sine.shape)]
            + [whole(seg_row.shape), whole(seg_col.shape)],
            out_specs=[qspec] * 3,
            scratch_shapes=[
                pltpu.VMEM((2, stacked, dim), LOW),
                pltpu.VMEM((2, stacked, dim), F32),
                pltpu.VMEM((2, stacked, 128), F32),
                pltpu.VMEM((2, stacked, 1), jnp.int32),
            ],
        ),
        out_shape=[jax.ShapeDtypeStruct((rows, qcols), kind) for kind in (LOW, F32, F32)],
        compiler_params=params(),
        cost_estimate=cost(2 * rows * total_rows * qcols * 2, 8 * rows * qcols * 2),
    )(info, qproj, kv, gain, cosine, sine, seg_row, seg_col)


def attend_back(info, qproj, kv, wide_out, logs, grad, gain, cosine, sine, seg_row, seg_col):
    rows, qcols = qproj.shape
    total_rows, kvcols = kv.shape
    dim = gain.shape[1]
    heads = kvcols // (2 * dim)
    wide = qcols // heads
    half = rows // 2
    stacked = half * (wide // dim)
    qspec, kspec = heads_spec(rows, wide), heads_spec(total_rows, 2 * dim)
    return pl.pallas_call(
        functools.partial(attend_back_kernel, half),
        grid_spec=pltpu.PrefetchScalarGridSpec(
            num_scalar_prefetch=1,
            grid=(heads,),
            in_specs=[qspec, kspec, qspec, qspec, qspec]
            + [whole(gain.shape), whole(cosine.shape), whole(sine.shape)]
            + [whole(seg_row.shape), whole(seg_col.shape)],
            out_specs=[qspec, kspec, pl.BlockSpec((1, 8, dim), lambda head, *_: (head, 0, 0))],
            scratch_shapes=[
                pltpu.VMEM((2, stacked, dim), LOW),
                pltpu.VMEM((2, stacked, dim), LOW),
                pltpu.VMEM((2, stacked, 1), jnp.int32),
                pltpu.VMEM((2, stacked, 1), F32),
                pltpu.VMEM((2, stacked, 1), F32),
                pltpu.VMEM((2, stacked, dim), F32),
                pltpu.VMEM((total_rows, 2 * dim), F32),
            ],
        ),
        out_shape=[
            jax.ShapeDtypeStruct((rows, qcols), LOW),
            jax.ShapeDtypeStruct((total_rows, kvcols), LOW),
            jax.ShapeDtypeStruct((heads, 8, dim), F32),
        ],
        compiler_params=params(),
        cost_estimate=cost(5 * rows * total_rows * qcols, 8 * rows * qcols * 4),
    )(info, qproj, kv, wide_out, logs, grad, gain, cosine, sine, seg_row, seg_col)


def key_forward(proj, gain, cosine, sine):
    return pl.pallas_call(
        key_forward_kernel,
        out_shape=jax.ShapeDtypeStruct(proj.shape, LOW),
        compiler_params=params(),
        cost_estimate=cost(10 * proj.size, 8 * proj.size),
    )(proj, gain, cosine, sine)


def key_backward(mine, other, proj, gain, cosine, sine):
    return pl.pallas_call(
        key_backward_kernel,
        out_shape=[
            jax.ShapeDtypeStruct(proj.shape, LOW),
            jax.ShapeDtypeStruct((8, gain.shape[1]), F32),
        ],
        compiler_params=params(),
        cost_estimate=cost(20 * proj.size, 12 * proj.size),
    )(mine, other, proj, gain, cosine, sine)


def feed_kernel(inputs, gate, up, dproduct, product, dgate, dup, dinputs, total):
    step = pl.program_id(0)
    gate_in = dot_plain(inputs[...], gate[...])
    up_in = dot_plain(inputs[...], up[...])
    sigmoid = 1.0 / (1.0 + jnp.exp(-gate_in))
    active = gate_in * sigmoid
    product[...] = (active * up_in).astype(LOW)
    grad = dproduct[...]
    dgate_low = (grad * up_in * sigmoid * (1.0 + gate_in * (1.0 - sigmoid))).astype(LOW)
    dup_low = (grad * active).astype(LOW)
    dgate[...] = dgate_low
    dup[...] = dup_low
    part = dot_right_t(dgate_low, gate[...]) + dot_right_t(dup_low, up[...])

    @pl.when(step == 0)
    def _():
        total[...] = part

    @pl.when(step > 0)
    def _():
        total[...] += part

    @pl.when(step == pl.num_programs(0) - 1)
    def _():
        dinputs[...] = total[...].astype(LOW)


def feed(inputs, gate, up, dproduct):
    rows, width = inputs.shape
    units = gate.shape[1]
    tile = min(256, units)
    wspec = pl.BlockSpec((width, tile), lambda step: (0, step))
    tspec = pl.BlockSpec((rows, tile), lambda step: (0, step))
    return pl.pallas_call(
        feed_kernel,
        grid=(units // tile,),
        in_specs=[whole((rows, width)), wspec, wspec, tspec],
        out_specs=[tspec, tspec, tspec, whole((rows, width))],
        out_shape=[jax.ShapeDtypeStruct((rows, units), LOW)] * 3 + [jax.ShapeDtypeStruct((rows, width), LOW)],
        scratch_shapes=[pltpu.VMEM((rows, width), F32)],
        compiler_params=params(),
        cost_estimate=cost(8 * rows * width * units, 4 * width * units + 10 * rows * units),
    )(inputs, gate, up, dproduct)


def shards(
    hidden_in,
    segments,
    cotangent,
    attn_gain,
    query_weight,
    key_weight,
    value_weight,
    output_weight,
    qnorm_gain,
    knorm_gain,
    ffn_gain,
    gate_weight,
    up_weight,
    down_weight,
):
    is_staged = lax.axis_size("fsdp") == 2 and lax.axis_size("context") == 4
    gather_fast = staged_gather if is_staged else gather_rows
    scatter_fast = staged_scatter if is_staged else scatter_rows
    head_dim = qnorm_gain.shape[0]
    local_rows, width = hidden_in.shape
    shard_rows = query_weight.shape[0]
    pieces = lax.axis_size("context")
    total_rows = local_rows * pieces
    half_rows = local_rows // 2
    value_heads = key_weight.shape[1] // head_dim
    qcols = query_weight.shape[1]
    kcols = key_weight.shape[1]

    def mixed(keys, values):
        parts = []
        for head in range(value_heads):
            spot = slice(head * head_dim, (head + 1) * head_dim)
            parts += [keys[:, spot], values[:, spot]]
        return jnp.concatenate(parts, axis=1)

    def unmixed(both, which):
        starts = [(2 * head + which) * head_dim for head in range(value_heads)]
        return jnp.concatenate([both[:, at : at + head_dim] for at in starts], axis=1)

    gain_row = jnp.concatenate([attn_gain, ffn_gain])[None, :]
    gain_pad = jnp.pad(gain_row, ((0, 15), (0, 2 * kcols - 2 * shard_rows)))
    kv_shard = jnp.concatenate([mixed(key_weight, value_weight), gain_pad])
    kv_ext = gather_fast(kv_shard).reshape(-1, shard_rows + 16, 2 * kcols)
    query_full = gather_fast(query_weight)
    out_full = gather_fast(output_weight)
    kv_full = kv_ext[:, :shard_rows].reshape(-1, 2 * kcols)
    blocks = staged_blocks() if is_staged else jnp.zeros((1,), jnp.int32)
    count = blocks.shape[0]
    gain_one = kv_ext[:, shard_rows, :shard_rows].astype(F32).reshape(count, -1)
    gain_two = kv_ext[:, shard_rows, shard_rows : 2 * shard_rows].astype(F32).reshape(count, -1)
    gate_full = gather_rows(gate_weight)

    me = lax.axis_index("context")
    last = 2 * pieces - 1
    spots = []
    for block in range(2 * pieces):
        owner = block if block < pieces else last - block
        spots.append(2 * (owner ^ me) + (0 if block < pieces else 1))
    info = jnp.stack([me, last - me] + spots).astype(jnp.int32)
    ramp = jnp.arange(half_rows, dtype=jnp.int32)
    positions = jnp.concatenate([me * half_rows + ramp, (last - me) * half_rows + ramp])
    seg_col = jnp.concatenate(
        [
            lax.dynamic_slice_in_dim(segments[0], block * half_rows, half_rows)
            for block in (me, last - me)
        ]
    )[:, None]
    half_dim = head_dim // 2
    inverse = THETA ** (-(jnp.arange(half_dim).astype(F32) * 2.0 / head_dim))
    angles = positions.astype(F32)[:, None] * inverse[None, :]
    cosine = jnp.cos(angles)
    sine = jnp.sin(angles)
    cosine = jnp.concatenate([cosine, cosine], axis=1)
    sine = jnp.concatenate([-sine, sine], axis=1)
    qgain = qnorm_gain.astype(F32)[None, :]
    kgain = knorm_gain.astype(F32)[None, :]

    (inputs_one,) = row_call(first_norm_kernel, blocks, [hidden_in], gain_one, [LOW])
    kv_proj = dot_plain(inputs_one, kv_full)
    kv_own = key_forward(kv_proj, kgain, cosine, sine)
    kv_across = swap_context(kv_own, 2)
    kv_all = jnp.concatenate([kv_own, swap_context(kv_own, 1), kv_across, swap_context(kv_across, 1)])
    query_proj = dot_plain(inputs_one, query_full)
    up_shard, gate_full, query_proj = tie(up_weight, gate_full, query_proj)
    up_full = gather_rows(up_shard)
    attended, attended_wide, logs = attend(
        info, query_proj, kv_all, qgain, cosine, sine, segments, seg_col
    )
    down_shard, up_full, attended = tie(down_weight, up_full, attended)
    down_full = gather_rows(down_shard)
    attn_out = sum_tensor(dot_right_t(attended, out_full))
    dproduct = dot_plain(cotangent, down_full)
    attn_out, dproduct = tie(attn_out, dproduct)
    middle, inputs_two, inputs_two_staged = row_call(
        second_norm_kernel, blocks, [hidden_in, attn_out], gain_two, [F32, LOW, LOW]
    )
    product, dgate, dup_low, dnormed_two_part = feed(inputs_two, gate_full, up_full, dproduct)
    dnormed_two = sum_tensor(dnormed_two_part)

    ffn_part = dot_right_t(product, down_full).astype(LOW)
    down_own = scatter_rows(dot_left_t(cotangent, product))
    gate_own = scatter_fast(dot_left_t(inputs_two_staged, dgate).astype(LOW))
    up_own = scatter_fast(dot_left_t(inputs_two_staged, dup_low).astype(LOW))
    gain_two_part = jnp.sum(dnormed_two_part.astype(F32) * inputs_two.astype(F32), axis=0)
    dnormed_two, ffn_part, gate_own, up_own = tie(dnormed_two, ffn_part, gate_own, up_own)
    ffn_out = sum_tensor(ffn_part)

    dmiddle, dattn = row_call(
        second_back_kernel, blocks, [dnormed_two, middle, cotangent], gain_two, [F32, LOW]
    )
    dattended = dot_plain(dattn, out_full).astype(LOW)
    dquery, dkv_part, qnorm_parts = attend_back(
        info, query_proj, kv_all, attended_wide, logs, dattended, qgain, cosine, sine, segments, seg_col
    )
    dkv_part = dkv_part.reshape(pieces, local_rows, 2 * kcols)
    dkv_pair = add_low(dkv_part[0::2], swap_context(dkv_part[1::2], 1))
    dkv, knorm_parts = key_backward(
        dkv_pair[0], swap_context(dkv_pair[1], 2), kv_proj, kgain, cosine, sine
    )
    output_own = scatter_fast(dot_left_t(dattn, attended).astype(LOW))
    dnormed_one_part = (dot_right_t(dquery, query_full) + dot_right_t(dkv, kv_full)).astype(LOW)
    dnormed_one_part, ffn_out = tie(dnormed_one_part, ffn_out)
    output = (middle + ffn_out.astype(F32)).astype(LOW)
    dnormed_one = sum_tensor(dnormed_one_part)
    qkv_own = scatter_fast(dot_left_t(inputs_one, jnp.concatenate([dquery, dkv], axis=1)).astype(LOW))
    gain_one_part = jnp.sum(dnormed_one_part.astype(F32) * inputs_one.astype(F32), axis=0)
    if is_staged:
        onehot = (blocks[None, :] == jnp.arange(count, dtype=jnp.int32)[:, None]).astype(F32)
        gain_one_part = jnp.dot(
            onehot, gain_one_part.reshape(count, -1), precision=lax.Precision.HIGHEST
        ).reshape(-1)
    small = lax.psum(
        jnp.concatenate(
            [gain_one_part, gain_two_part, jnp.sum(qnorm_parts, axis=(0, 1)), jnp.sum(knorm_parts, axis=0)]
        ),
        ("fsdp", "context", "tensor"),
    )
    dnormed_one, small = tie(dnormed_one, small)
    (input_grad,) = row_call(
        first_back_kernel, blocks, [dnormed_one, hidden_in, dmiddle], gain_one, [F32]
    )
    own = attn_gain.shape[0]
    start = lax.axis_index(ROWS) * own
    gain_one_grad = lax.dynamic_slice_in_dim(small[:width], start, own) / attn_gain.astype(F32)
    gain_two_grad = lax.dynamic_slice_in_dim(small[width : 2 * width], start, own) / ffn_gain.astype(F32)
    qnorm_total = small[2 * width : 2 * width + head_dim]
    knorm_total = small[2 * width + head_dim :]
    qkv_own = qkv_own.astype(F32)
    return (
        output,
        input_grad,
        gain_one_grad,
        qkv_own[:, :qcols],
        unmixed(qkv_own[:, qcols:], 0),
        unmixed(qkv_own[:, qcols:], 1),
        output_own.astype(F32),
        qnorm_total,
        knorm_total,
        gain_two_grad,
        gate_own.astype(F32),
        up_own.astype(F32),
        down_own.astype(F32),
    )


def solution(mesh):
    in_specs = (
        P(("fsdp", "context"), None),
        P("fsdp", None),
        P(("fsdp", "context"), None),
        P(("fsdp", "context")),
        P(("fsdp", "context"), "tensor"),
        P(("fsdp", "context"), "tensor"),
        P(("fsdp", "context"), "tensor"),
        P(("fsdp", "context"), "tensor"),
        P(),
        P(),
        P(("fsdp", "context")),
        P(("fsdp", "context"), "tensor"),
        P(("fsdp", "context"), "tensor"),
        P(("fsdp", "context"), "tensor"),
    )
    out_specs = (
        P(("fsdp", "context"), None),
        P(("fsdp", "context"), None),
        P(("fsdp", "context")),
        P(("fsdp", "context"), "tensor"),
        P(("fsdp", "context"), "tensor"),
        P(("fsdp", "context"), "tensor"),
        P(("fsdp", "context"), "tensor"),
        P(),
        P(),
        P(("fsdp", "context")),
        P(("fsdp", "context"), "tensor"),
        P(("fsdp", "context"), "tensor"),
        P(("fsdp", "context"), "tensor"),
    )
    return jax.shard_map(shards, mesh=mesh, in_specs=in_specs, out_specs=out_specs, check_vma=False)
```

```python
import functools

import jax
import jax.numpy as jnp
from jax import lax
from jax.experimental import pallas as pl
from jax.experimental.pallas import tpu as pltpu
from jax.sharding import PartitionSpec as P

EPS = 1e-06
THETA = 1000000.0
ROWS = ("fsdp", "context")
LOW = jnp.bfloat16
F32 = jnp.float32
LOG2E = 1.4426950408889634
VMEM_BYTES = 56 * 1024 * 1024


def dot_plain(matrix_a, matrix_b):
    return jnp.dot(matrix_a, matrix_b, preferred_element_type=F32)


def dot_right_t(matrix_a, matrix_b):
    return lax.dot_general(matrix_a, matrix_b, (((1,), (1,)), ((), ())), preferred_element_type=F32)


def dot_left_t(matrix_a, matrix_b):
    return lax.dot_general(matrix_a, matrix_b, (((0,), (0,)), ((), ())), preferred_element_type=F32)


def tie(*items):
    return lax.optimization_barrier(items)


def rms_scale(values):
    return lax.rsqrt(jnp.mean(values * values, axis=-1, keepdims=True) + EPS)


def gather_rows(shard):
    return lax.all_gather(shard, ROWS, axis=0, tiled=True)


def scatter_rows(full):
    return lax.psum_scatter(full.astype(LOW), ROWS, scatter_dimension=0, tiled=True)


def sum_tensor(partial):
    return lax.psum(partial.astype(LOW), "tensor")


def add_low(mine, other):
    return (mine.astype(F32) + other.astype(F32)).astype(LOW)


def place(index):
    return index // 4, (index // 2) % 2, index % 2


def staged_pairs(step):
    pairs = []
    for index in range(8):
        x, y, core = place(index)
        if step == "core":
            core = 1 - core
        elif (step == "first") == (core == 0):
            x = 1 - x
        else:
            y = 1 - y
        pairs.append((index, x * 4 + y * 2 + core))
    return pairs


def staged(values, step):
    return lax.ppermute(values, ROWS, staged_pairs(step))


def staged_blocks():
    x, y, core = place(lax.axis_index(ROWS))
    blocks = []
    for step in range(8):
        d_core, d_second, d_first = step // 4, (step // 2) % 2, step % 2
        its_core = core ^ d_core
        its_x = x ^ jnp.where(its_core == 0, d_first, d_second)
        its_y = y ^ jnp.where(its_core == 0, d_second, d_first)
        blocks.append(its_x * 4 + its_y * 2 + its_core)
    return jnp.stack(blocks).astype(jnp.int32)


def staged_halves(shard):
    pair = jnp.concatenate([shard, staged(shard, "first")])
    quad = jnp.concatenate([pair, staged(pair, "second")])
    return [quad, staged(quad, "core")]


def staged_gather(shard):
    return jnp.concatenate(staged_halves(shard))


def staged_scatter(full):
    rows = full.shape[0] // 8
    quad = add_low(full[: 4 * rows], staged(full[4 * rows :], "core"))
    pair = add_low(quad[: 2 * rows], staged(quad[2 * rows :], "second"))
    return pair[:rows].astype(F32) + staged(pair[rows:], "first").astype(F32)


def sum_all(values):
    for axis in ("tensor", "context", "fsdp"):
        size = lax.axis_size(axis)
        if size & (size - 1):
            values = lax.psum(values, axis)
            continue
        bit = 1
        while bit < size:
            values = values + lax.ppermute(values, axis, [(index, index ^ bit) for index in range(size)])
            bit *= 2
    return values


def swap_context(values, bit):
    size = lax.axis_size("context")
    return lax.ppermute(values, "context", [(index, index ^ bit) for index in range(size)])


def params():
    return pltpu.CompilerParams(vmem_limit_bytes=VMEM_BYTES)


def cost(flops, moved):
    return pl.CostEstimate(flops=int(flops), bytes_accessed=int(moved), transcendentals=0)


def whole(shape):
    return pl.BlockSpec(shape, lambda *_: (0,) * len(shape))


def column(ids, step, width):
    return pl.ds(pl.multiple_of(ids[step] * width, width), width)


def stage_kernel(count, ids, values, staged_out):
    width = values.shape[1] // count
    for step in range(count):
        staged_out[:, step * width : (step + 1) * width] = values[:, column(ids, step, width)]


def by_rows(rows, body):
    def run(step, carry):
        body(pl.ds(pl.multiple_of(step * 16, 16), 16))
        return carry

    lax.fori_loop(0, rows // 16, run, 0, unroll=2)


def row_sum(parts):
    return jnp.sum(sum(parts), axis=-1, keepdims=True)


def scale_of(parts):
    size = len(parts) * parts[0].shape[1]
    return lax.rsqrt(row_sum([part * part for part in parts]) / size + EPS)


def second_norm_kernel(count, ids, hidden, attn, gain, middle, plain_out):
    width = hidden.shape[1] // count
    spots = [column(ids, step, width) for step in range(count)]

    def body(rows):
        parts = []
        for step in range(count):
            part = attn[rows, step * width : (step + 1) * width].astype(F32)
            parts.append(hidden[rows, spots[step]].astype(F32) + part)
            middle[rows, spots[step]] = parts[step]
        scale = scale_of(parts)
        for step in range(count):
            plain_out[rows, spots[step]] = (parts[step] * scale * gain[step : step + 1, :]).astype(LOW)

    by_rows(hidden.shape[0], body)


def output_kernel(count, ids, middle, ffn, out):
    width = middle.shape[1] // count
    for step in range(count):
        spot = column(ids, step, width)
        out[:, spot] = (middle[:, spot] + ffn[:, step * width : (step + 1) * width].astype(F32)).astype(LOW)


def second_back_kernel(count, ids, grad, middle, cotangent, gain, dmiddle, staged_out, gain_out):
    width = middle.shape[1] // count

    @pl.when(pl.program_id(0) == 0)
    def _():
        gain_out[...] = jnp.zeros_like(gain_out)

    spots = [column(ids, step, width) for step in range(count)]

    def body(rows):
        parts = [middle[rows, spot] for spot in spots]
        raw = [grad[rows, spot].astype(F32) for spot in spots]
        grads = [raw[step] * gain[step : step + 1, :] for step in range(count)]
        scale = scale_of(parts)
        mean = row_sum([one * two for one, two in zip(parts, grads)]) * scale * scale / middle.shape[1]
        for step in range(count):
            term = raw[step] * parts[step] * scale
            gain_out[:, spots[step]] += term[:8] + term[8:]
            part = cotangent[rows, spots[step]].astype(F32) + scale * (grads[step] - parts[step] * mean)
            dmiddle[rows, spots[step]] = part
            staged_out[rows, step * width : (step + 1) * width] = part.astype(LOW)

    by_rows(middle.shape[0], body)


def first_back_kernel(count, ids, grad, hidden, dmiddle, gain, out):
    width = hidden.shape[1] // count
    spots = [column(ids, step, width) for step in range(count)]

    def body(rows):
        parts = [hidden[rows, spot].astype(F32) for spot in spots]
        grads = [
            grad[rows, step * width : (step + 1) * width].astype(F32) * gain[step : step + 1, :]
            for step in range(count)
        ]
        scale = scale_of(parts)
        mean = row_sum([one * two for one, two in zip(parts, grads)]) * scale * scale / hidden.shape[1]
        for step in range(count):
            out[rows, spots[step]] = dmiddle[rows, spots[step]] + scale * (grads[step] - parts[step] * mean)

    by_rows(hidden.shape[0], body)


def row_call(kernel, ids, arrays, out_types, gain=None, sums=False, brief=False):
    rows, width = arrays[0].shape
    tile = min(128, rows)
    spec = pl.BlockSpec((tile, width), lambda step, *_: (step, 0))
    moved = sum(item.size * item.dtype.itemsize for item in arrays) + sum(
        rows * width * jnp.dtype(kind).itemsize for kind in out_types
    )
    gains = [] if gain is None else [gain]
    return pl.pallas_call(
        functools.partial(kernel, ids.shape[0]),
        grid_spec=pltpu.PrefetchScalarGridSpec(
            num_scalar_prefetch=1,
            grid=(rows // tile,),
            in_specs=[spec] * len(arrays) + [whole(item.shape) for item in gains],
            out_specs=[spec] * len(out_types) + [whole((8, width))] * sums,
        ),
        out_shape=[jax.ShapeDtypeStruct((rows, width), kind) for kind in out_types]
        + [jax.ShapeDtypeStruct((8, width), F32)] * sums,
        compiler_params=params(),
        cost_estimate=cost(0, rows * width) if brief else cost(10 * rows * width, moved),
    )(ids, *arrays, *gains)


def rotate(values, cosine, sine):
    return values * cosine + pltpu.roll(values, values.shape[1] // 2, 1) * sine


def head_forward(proj, gain, cosine, sine):
    scale = rms_scale(proj)
    unit = proj * scale
    return rotate(unit * gain, cosine, sine).astype(LOW), unit, scale


def head_backward(grad, unit, scale, gain, cosine, sine):
    turned = rotate(grad.astype(LOW).astype(F32), cosine, -sine)
    scaled = turned * gain
    back = scale * (scaled - unit * jnp.mean(scaled * unit, axis=-1, keepdims=True))
    rows, width = grad.shape
    return back.astype(LOW), jnp.sum((turned * unit).reshape(rows // 8, 8, width), axis=0)


def opening_kernel(count, parts_in, ids, hidden, *refs):
    weights, refs = refs[:parts_in], refs[parts_in:]
    kgain, cosine, sine, normed, proj, qproj, out, out_weights = refs
    width = hidden.shape[1] // count
    each = count // parts_in
    high = weights[0].shape[0] // each
    dim = kgain.shape[1]
    spots = [column(ids, step, width) for step in range(count)]

    def part_of(step):
        return weights[step // each], (step % each) * high

    def body(rows):
        parts = [hidden[rows, spot].astype(F32) for spot in spots]
        scale = scale_of(parts)
        for step in range(count):
            source, at = part_of(step)
            gain = source[at + width : at + width + 16, :width].astype(F32)[:1]
            normed[rows, step * width : (step + 1) * width] = (parts[step] * scale * gain).astype(LOW)

    by_rows(hidden.shape[0], body)
    kvcols, qcols = proj.shape[1], qproj.shape[1]

    def project(cols):
        total = jnp.zeros((hidden.shape[0], cols.stop - cols.start), F32)
        for step in range(count):
            source, at = part_of(step)
            total = total + dot_plain(normed[:, step * width : (step + 1) * width], source[at : at + width, cols])
        return total

    total = project(slice(0, kvcols))
    proj[...] = total
    for head in range(kvcols // (2 * dim)):
        at = 2 * head * dim
        out[:, at : at + dim] = head_forward(total[:, at : at + dim], kgain[...], cosine[...], sine[...])[0]
        out[:, at + dim : at + 2 * dim] = total[:, at + dim : at + 2 * dim].astype(LOW)
    qproj[...] = project(slice(kvcols, kvcols + qcols))

    @pl.when(pl.program_id(0) == 0)
    def _():
        for step in range(count):
            source, at = part_of(step)
            far = slice(kvcols + qcols, kvcols + qcols + out_weights.shape[1])
            out_weights[step * width : (step + 1) * width, :] = source[at : at + width, far]


def key_backward_kernel(mine, other, proj, gain, cosine, sine, out, norm_out):
    dim = gain.shape[1]
    total = jnp.zeros(norm_out.shape, F32)
    for head in range(proj.shape[1] // (2 * dim)):
        at = 2 * head * dim
        scale = rms_scale(proj[:, at : at + dim])
        unit = proj[:, at : at + dim] * scale
        grad = mine[:, at : at + dim].astype(F32) + other[:, at : at + dim].astype(F32)
        back, norm = head_backward(grad, unit, scale, gain[...], cosine[...], sine[...])
        total = total + norm
        out[:, at : at + dim] = back
        spot = slice(at + dim, at + 2 * dim)
        out[:, spot] = (mine[:, spot].astype(F32) + other[:, spot].astype(F32)).astype(LOW)
    norm_out[...] = total


def pair_of(info, step):
    first = info[0]
    late = step > first
    piece = jnp.where(late, 1, 0)
    key_block = jnp.where(late, step - first - 1, step)
    query_block = jnp.where(late, info[1], first)
    return piece, key_block, query_block, info[2 + key_block]


def allowed_pair(shape, half, query_block, key_block, query_seg, key_seg):
    row = lax.rem(lax.broadcasted_iota(jnp.int32, shape, 0), half)
    col = lax.broadcasted_iota(jnp.int32, shape, 1)
    return (col - row <= (query_block - key_block) * half) & (query_seg == key_seg)


def load_pieces(pieces, kv):
    rows = pieces[0].shape[0]
    for place_at, piece in enumerate(pieces):
        kv[place_at * rows : (place_at + 1) * rows, :] = piece[...]


def attend_kernel(half, count, info, qproj, weights, *refs):
    pieces, (gain, cosine, sine, seg_row, seg_col), refs = refs[:count], refs[count : count + 5], refs[count + 5 :]
    out, out_wide, log_out, part_out, qs, acc, total, segq, kv, part_sum = refs
    load_pieces(pieces, kv)
    dim = gain.shape[1]
    group = qproj.shape[1] // dim
    pairs = info.shape[0] - 1
    factor = LOG2E * dim ** (-0.5)
    for head in range(group):
        cols = slice(head * dim, (head + 1) * dim)
        query = head_forward(qproj[:, cols], gain[...], cosine[...], sine[...])[0]
        for piece in range(2):
            spot = slice(head * half, (head + 1) * half)
            rows = slice(piece * half, (piece + 1) * half)
            qs[piece, spot, :] = query[rows]
            segq[piece, spot, :] = seg_col[rows, :]
    acc[...] = jnp.zeros_like(acc)
    total[...] = jnp.zeros_like(total)
    for step in range(pairs):
        piece, key_block, query_block, spot = pair_of(info, step)
        rows = pl.ds(pl.multiple_of(spot * half, half), half)
        scores = dot_right_t(qs[piece], kv[rows, :dim])
        key_seg = seg_row[:, pl.ds(pl.multiple_of(key_block * half, half), half)]
        allowed = allowed_pair(scores.shape, half, query_block, key_block, segq[piece], key_seg)
        weight = jnp.where(allowed, jnp.exp2(scores * factor), 0.0)
        total[piece] += sum(weight[:, at : at + 128] for at in range(0, half, 128))
        acc[piece] += dot_plain(weight.astype(LOW), kv[rows, dim:])
    for piece in range(2):
        sums = jnp.sum(total[piece], axis=-1, keepdims=True)
        result = acc[piece] / sums
        logs = jnp.broadcast_to(jnp.log2(sums), result.shape)
        for head in range(group):
            cols = slice(head * dim, (head + 1) * dim)
            rows = slice(piece * half, (piece + 1) * half)
            part = result[head * half : (head + 1) * half]
            out[rows, cols] = part.astype(LOW)
            out_wide[rows, cols] = part
            log_out[rows, cols] = logs[head * half : (head + 1) * half]
    here = pl.program_id(0)

    @pl.when(here == 0)
    def _():
        part_sum[...] = dot_right_t(out[...], weights[...])

    @pl.when(here > 0)
    def _():
        part_sum[...] += dot_right_t(out[...], weights[...])

    @pl.when(here == pl.num_programs(0) - 1)
    def _():
        part_out[...] = part_sum[...].astype(LOW)


def attend_back_kernel(half, count, info, qproj, wide, logs, grad, *refs):
    pieces, (gain, cosine, sine, seg_row, seg_col), refs = refs[:count], refs[count : count + 5], refs[count + 5 :]
    dq_out, keep_out, send_out, norm_out, qs, gs, segq, ls, ds, dq, dkv, kv = refs
    load_pieces(pieces, kv)
    dim = gain.shape[1]
    group = qproj.shape[1] // dim
    pairs = info.shape[0] - 1
    plain = dim ** (-0.5)
    factor = LOG2E * plain
    for head in range(group):
        cols = slice(head * dim, (head + 1) * dim)
        query = head_forward(qproj[:, cols], gain[...], cosine[...], sine[...])[0]
        delta = jnp.sum(grad[:, cols].astype(F32) * wide[:, cols], axis=-1, keepdims=True)
        for piece in range(2):
            spot = slice(head * half, (head + 1) * half)
            rows = slice(piece * half, (piece + 1) * half)
            qs[piece, spot, :] = query[rows]
            gs[piece, spot, :] = grad[rows, cols]
            segq[piece, spot, :] = seg_col[rows, :]
            ls[piece, spot, :] = logs[rows, head * dim : head * dim + 1]
            ds[piece, spot, :] = delta[rows]
    dq[...] = jnp.zeros_like(dq)
    dkv[...] = jnp.zeros_like(dkv)
    for step in range(pairs):
        piece, key_block, query_block, spot = pair_of(info, step)
        rows = pl.ds(pl.multiple_of(spot * half, half), half)
        query, outer = qs[piece], gs[piece]
        scores = dot_right_t(query, kv[rows, :dim])
        key_seg = seg_row[:, pl.ds(pl.multiple_of(key_block * half, half), half)]
        allowed = allowed_pair(scores.shape, half, query_block, key_block, segq[piece], key_seg)
        prob = jnp.where(allowed, jnp.exp2(scores * factor - ls[piece]), 0.0)
        dprob = dot_right_t(outer, kv[rows, dim:])
        dscores = (prob * (dprob - ds[piece])).astype(LOW)
        dq[piece] += dot_plain(dscores, kv[rows, :dim])
        dkv[rows, :dim] += dot_left_t(dscores, query)
        dkv[rows, dim:] += dot_left_t(prob.astype(LOW), outer)
    rows = 2 * half
    for at in range(count):
        target = send_out if at % 2 else keep_out
        spot, low = slice(at // 2 * rows, (at // 2 + 1) * rows), slice(at * rows, (at + 1) * rows)
        target[spot, :dim] = (dkv[low, :dim] * plain).astype(LOW)
        target[spot, dim:] = dkv[low, dim:].astype(LOW)
    total = jnp.zeros(norm_out.shape[1:], F32)
    for head in range(group):
        cols = slice(head * dim, (head + 1) * dim)
        scale = rms_scale(qproj[:, cols])
        unit = qproj[:, cols] * scale
        grads = jnp.concatenate([dq[piece, head * half : (head + 1) * half, :] for piece in range(2)]) * plain
        back, norm = head_backward(grads, unit, scale, gain[...], cosine[...], sine[...])
        total = total + norm
        dq_out[:, cols] = back
    norm_out[0] = total


def heads_spec(rows, width):
    return pl.BlockSpec((rows, width), lambda head, *_: (0, head))


def attend(info, qproj, weights, pieces, gain, cosine, sine, seg_row, seg_col):
    rows, qcols = qproj.shape
    count, kvcols = len(pieces), pieces[0].shape[1]
    dim = gain.shape[1]
    heads = kvcols // (2 * dim)
    wide = qcols // heads
    half = rows // 2
    stacked = half * (wide // dim)
    qspec, kspec = heads_spec(rows, wide), heads_spec(rows, 2 * dim)
    tables = (gain, cosine, sine, seg_row, seg_col)
    return pl.pallas_call(
        functools.partial(attend_kernel, half, count),
        grid_spec=pltpu.PrefetchScalarGridSpec(
            num_scalar_prefetch=1,
            grid=(heads,),
            in_specs=[qspec, heads_spec(weights.shape[0], wide)]
            + [kspec] * count
            + [whole(item.shape) for item in tables],
            out_specs=[qspec] * 3 + [whole((rows, weights.shape[0]))],
            scratch_shapes=[
                pltpu.VMEM((2, stacked, dim), LOW),
                pltpu.VMEM((2, stacked, dim), F32),
                pltpu.VMEM((2, stacked, 128), F32),
                pltpu.VMEM((2, stacked, 1), jnp.int32),
                pltpu.VMEM((count * rows, 2 * dim), LOW),
                pltpu.VMEM((rows, weights.shape[0]), F32),
            ],
        ),
        out_shape=[jax.ShapeDtypeStruct((rows, qcols), kind) for kind in (LOW, F32, F32)]
        + [jax.ShapeDtypeStruct((rows, weights.shape[0]), LOW)],
        compiler_params=params(),
        cost_estimate=cost(2 * rows * count * rows * qcols * 2, 8 * rows * qcols * 2),
    )(info, qproj, weights, *pieces, *tables)


def attend_back(info, qproj, wide_out, logs, grad, pieces, gain, cosine, sine, seg_row, seg_col):
    rows, qcols = qproj.shape
    count, kvcols = len(pieces), pieces[0].shape[1]
    dim = gain.shape[1]
    heads = kvcols // (2 * dim)
    wide = qcols // heads
    half = rows // 2
    stacked = half * (wide // dim)
    qspec, kspec = heads_spec(rows, wide), heads_spec(rows, 2 * dim)
    part = heads_spec(count // 2 * rows, 2 * dim)
    tables = (gain, cosine, sine, seg_row, seg_col)
    return pl.pallas_call(
        functools.partial(attend_back_kernel, half, count),
        grid_spec=pltpu.PrefetchScalarGridSpec(
            num_scalar_prefetch=1,
            grid=(heads,),
            in_specs=[qspec] * 4 + [kspec] * count + [whole(item.shape) for item in tables],
            out_specs=[qspec, part, part, pl.BlockSpec((1, 8, dim), lambda head, *_: (head, 0, 0))],
            scratch_shapes=[
                pltpu.VMEM((2, stacked, dim), LOW),
                pltpu.VMEM((2, stacked, dim), LOW),
                pltpu.VMEM((2, stacked, 1), jnp.int32),
                pltpu.VMEM((2, stacked, 1), F32),
                pltpu.VMEM((2, stacked, 1), F32),
                pltpu.VMEM((2, stacked, dim), F32),
                pltpu.VMEM((count * rows, 2 * dim), F32),
                pltpu.VMEM((count * rows, 2 * dim), LOW),
            ],
        ),
        out_shape=[
            jax.ShapeDtypeStruct((rows, qcols), LOW),
            jax.ShapeDtypeStruct((count // 2 * rows, kvcols), LOW),
            jax.ShapeDtypeStruct((count // 2 * rows, kvcols), LOW),
            jax.ShapeDtypeStruct((heads, 8, dim), F32),
        ],
        compiler_params=params(),
        cost_estimate=cost(0, rows * qcols),
    )(info, qproj, wide_out, logs, grad, *pieces, *tables)


def assemble_kernel(dim, key, value, query, output, gains, out):
    rows, kcols = key.shape
    qcols = query.shape[1]
    for head in range(kcols // dim):
        spot = slice(head * dim, (head + 1) * dim)
        out[:rows, 2 * head * dim : (2 * head + 1) * dim] = key[:, spot]
        out[:rows, (2 * head + 1) * dim : (2 * head + 2) * dim] = value[:, spot]
    out[:rows, 2 * kcols : 2 * kcols + qcols] = query[...]
    out[:rows, 2 * kcols + qcols :] = output[...]
    out[rows:, :] = jnp.zeros((16, out.shape[1]), LOW)
    out[rows:, : gains.shape[1]] = gains[...]


def assemble(key, value, query, output, gain_one, gain_two, dim):
    gains = jnp.pad(jnp.concatenate([gain_one, gain_two])[None, :], ((0, 15), (0, 0)))
    cols = 2 * key.shape[1] + query.shape[1] + output.shape[1]
    return pl.pallas_call(
        functools.partial(assemble_kernel, dim),
        out_shape=jax.ShapeDtypeStruct((key.shape[0] + 16, cols), LOW),
        compiler_params=params(),
        cost_estimate=cost(0, 4 * key.shape[0] * cols),
    )(key, value, query, output, gains)


def opening(ids, hidden, halves, kvcols, qcols, kgain, cosine, sine):
    rows, width = hidden.shape
    tile = min(256, rows)
    shapes = [(width, LOW), (kvcols, F32), (qcols, F32), (kvcols, LOW)]

    def tiled(cols):
        return pl.BlockSpec((tile, cols), lambda step, *_: (step, 0))

    return pl.pallas_call(
        functools.partial(opening_kernel, ids.shape[0], len(halves)),
        grid_spec=pltpu.PrefetchScalarGridSpec(
            num_scalar_prefetch=1,
            grid=(rows // tile,),
            in_specs=[tiled(width)]
            + [whole(item.shape) for item in halves]
            + [whole(kgain.shape), tiled(cosine.shape[1]), tiled(sine.shape[1])],
            out_specs=[tiled(cols) for cols, _ in shapes] + [whole((width, qcols))],
        ),
        out_shape=[jax.ShapeDtypeStruct((rows, cols), kind) for cols, kind in shapes]
        + [jax.ShapeDtypeStruct((width, qcols), LOW)],
        compiler_params=params(),
        cost_estimate=cost(2 * rows * width * (kvcols + qcols), 4 * rows * width + 2 * width * kvcols),
    )(ids, hidden, *halves, kgain, cosine, sine)


def key_backward(mine, other, proj, gain, cosine, sine):
    return pl.pallas_call(
        key_backward_kernel,
        out_shape=[
            jax.ShapeDtypeStruct(proj.shape, LOW),
            jax.ShapeDtypeStruct((8, gain.shape[1]), F32),
        ],
        compiler_params=params(),
        cost_estimate=cost(0, proj.size),
    )(mine, other, proj, gain, cosine, sine)


def feed_kernel(inputs, gate, up, dproduct, product, dgate, dup, dinputs, total):
    step = pl.program_id(0)
    gate_in = dot_plain(inputs[...], gate[...])
    up_in = dot_plain(inputs[...], up[...])
    sigmoid = 1.0 / (1.0 + jnp.exp(-gate_in))
    active = gate_in * sigmoid
    product[...] = (active * up_in).astype(LOW)
    grad = dproduct[...]
    dgate_low = (grad * up_in * sigmoid * (1.0 + gate_in * (1.0 - sigmoid))).astype(LOW)
    dup_low = (grad * active).astype(LOW)
    dgate[...] = dgate_low
    dup[...] = dup_low
    part = dot_right_t(dgate_low, gate[...]) + dot_right_t(dup_low, up[...])

    @pl.when(step == 0)
    def _():
        total[...] = part

    @pl.when(step > 0)
    def _():
        total[...] += part

    @pl.when(step == pl.num_programs(0) - 1)
    def _():
        dinputs[...] = total[...].astype(LOW)


def feed(inputs, gate_up, dproduct):
    rows, width = inputs.shape
    units = dproduct.shape[1]
    tile = min(256, units)
    count = units // tile
    gspec = pl.BlockSpec((width, tile), lambda step: (0, step))
    uspec = pl.BlockSpec((width, tile), lambda step: (0, step + count))
    tspec = pl.BlockSpec((rows, tile), lambda step: (0, step))
    return pl.pallas_call(
        feed_kernel,
        grid=(count,),
        in_specs=[whole((rows, width)), gspec, uspec, tspec],
        out_specs=[tspec, tspec, tspec, whole((rows, width))],
        out_shape=[jax.ShapeDtypeStruct((rows, units), LOW)] * 3 + [jax.ShapeDtypeStruct((rows, width), LOW)],
        scratch_shapes=[pltpu.VMEM((rows, width), F32)],
        compiler_params=params(),
        cost_estimate=cost(8 * rows * width * units, 4 * width * units + 10 * rows * units),
    )(inputs, gate_up, gate_up, dproduct)


def shards(
    hidden_in,
    segments,
    cotangent,
    attn_gain,
    query_weight,
    key_weight,
    value_weight,
    output_weight,
    qnorm_gain,
    knorm_gain,
    ffn_gain,
    gate_weight,
    up_weight,
    down_weight,
):
    is_staged = lax.axis_size("fsdp") == 2 and lax.axis_size("context") == 4
    gather_fast = staged_gather if is_staged else gather_rows
    scatter_fast = staged_scatter if is_staged else scatter_rows
    head_dim = qnorm_gain.shape[0]
    local_rows, width = hidden_in.shape
    shard_rows = query_weight.shape[0]
    pieces = lax.axis_size("context")
    total_rows = local_rows * pieces
    half_rows = local_rows // 2
    value_heads = key_weight.shape[1] // head_dim
    qcols = query_weight.shape[1]
    kcols = key_weight.shape[1]

    def unmixed(both, which):
        starts = [(2 * head + which) * head_dim for head in range(value_heads)]
        return jnp.concatenate([both[:, at : at + head_dim] for at in starts], axis=1)

    blocks = staged_blocks() if is_staged else jnp.zeros((1,), jnp.int32)
    count = blocks.shape[0]
    near = 2 * kcols + qcols
    first_shard = assemble(key_weight, value_weight, query_weight, output_weight, attn_gain, ffn_gain, head_dim)
    halves = staged_halves(first_shard) if is_staged else [gather_rows(first_shard)]

    def without_gains():
        parts = [half.reshape(-1, shard_rows + 16, half.shape[1])[:, :shard_rows] for half in halves]
        return jnp.concatenate([part.reshape(-1, part.shape[2]) for part in parts])

    gain_rows = [half.reshape(-1, shard_rows + 16, half.shape[1])[:, shard_rows] for half in halves]
    gain_rows = jnp.concatenate(gain_rows).astype(F32)
    gain_one = gain_rows[:, :shard_rows].reshape(count, -1)
    gain_two = gain_rows[:, shard_rows : 2 * shard_rows].reshape(count, -1)
    opening_halves = halves
    if not is_staged:
        gain_tail = jnp.pad(gain_one.astype(LOW), ((0, 15), (0, 0)))
        far = max(first_shard.shape[1], width)
        opening_halves = [
            jnp.concatenate(
                [jnp.pad(item, ((0, 0), (0, far - item.shape[1]))) for item in (without_gains(), gain_tail)]
            )
        ]

    me = lax.axis_index("context")
    last = 2 * pieces - 1
    spots = []
    for block in range(2 * pieces):
        owner = block if block < pieces else last - block
        spots.append(2 * (owner ^ me) + (0 if block < pieces else 1))
    info = jnp.stack([me, last - me] + spots).astype(jnp.int32)
    ramp = jnp.arange(half_rows, dtype=jnp.int32)
    positions = jnp.concatenate([me * half_rows + ramp, (last - me) * half_rows + ramp])
    seg_col = jnp.concatenate(
        [
            lax.dynamic_slice_in_dim(segments[0], block * half_rows, half_rows)
            for block in (me, last - me)
        ]
    )[:, None]
    half_dim = head_dim // 2
    inverse = THETA ** (-(jnp.arange(half_dim).astype(F32) * 2.0 / head_dim))
    angles = positions.astype(F32)[:, None] * inverse[None, :]
    cosine = jnp.cos(angles)
    sine = jnp.sin(angles)
    cosine = jnp.concatenate([cosine, cosine], axis=1)
    sine = jnp.concatenate([-sine, sine], axis=1)
    qgain = qnorm_gain.astype(F32)[None, :]
    kgain = knorm_gain.astype(F32)[None, :]

    (cot_staged,) = row_call(stage_kernel, blocks, [cotangent], [LOW])
    inputs_one, kv_proj, query_proj, kv_own, out_full = opening(
        blocks, hidden_in, opening_halves, 2 * kcols, qcols, kgain, cosine, sine
    )
    kv_across = swap_context(kv_own, 2)
    kv_pieces = [kv_own, swap_context(kv_own, 1), kv_across, swap_context(kv_across, 1)]
    gate_up_shard, kv_proj = tie(jnp.concatenate([gate_weight, up_weight], axis=1), kv_proj)
    gate_up = gather_rows(gate_up_shard)
    attended, attended_wide, logs, attn_part = attend(
        info, query_proj, out_full, kv_pieces, qgain, cosine, sine, segments, seg_col
    )
    down_shard, logs = tie(down_weight, logs)
    down_full = gather_fast(down_shard)
    attn_out = sum_tensor(attn_part)
    dproduct = dot_plain(cot_staged, down_full)
    near_full = without_gains()[:, :near]
    attn_out, dproduct, near_full = tie(attn_out, dproduct, near_full)
    middle, inputs_two = row_call(second_norm_kernel, blocks, [hidden_in, attn_out], [F32, LOW], gain_two)
    product, dgate, dup_low, dnormed_two_part = feed(inputs_two, gate_up, dproduct)
    dnormed_two = sum_tensor(dnormed_two_part)

    ffn_part = dot_right_t(product, down_full).astype(LOW)
    down_own = scatter_rows(dot_left_t(cotangent, product))
    grad_gate = dot_left_t(inputs_two, dgate).astype(LOW)
    grad_up = dot_left_t(inputs_two, dup_low).astype(LOW)
    dnormed_two, ffn_part, grad_gate, grad_up = tie(dnormed_two, ffn_part, grad_gate, grad_up)
    ffn_out = sum_tensor(ffn_part)
    dmiddle, dattn, gain_two_sums = row_call(
        second_back_kernel, blocks, [dnormed_two, middle, cotangent], [F32, LOW], gain_two, True, True
    )
    gain_two_part = jnp.sum(gain_two_sums, axis=0) / lax.axis_size("tensor")
    dattended = dot_plain(dattn, out_full).astype(LOW)
    dquery, dkv_keep, dkv_send, qnorm_parts = attend_back(
        info, query_proj, attended_wide, logs, dattended, kv_pieces, qgain, cosine, sine, segments, seg_col
    )
    grad_gate, down_own, qnorm_parts = tie(grad_gate, down_own, qnorm_parts)
    gate_own = scatter_rows(grad_gate)
    dkv_pair = add_low(dkv_keep, swap_context(dkv_send, 1))
    dkv, knorm_parts = key_backward(
        dkv_pair[:local_rows], swap_context(dkv_pair[local_rows:], 2), kv_proj, kgain, cosine, sine
    )
    output_own = scatter_fast(dot_left_t(dattn, attended).astype(LOW))
    dqkv = jnp.concatenate([dkv, dquery], axis=1)
    dnormed_one_part = dot_right_t(dqkv, near_full).astype(LOW)
    later_part, ffn_out = tie(dnormed_one_part, ffn_out)
    dnormed_one = sum_tensor(later_part)
    grad_up, gate_own, ffn_out = tie(grad_up, gate_own, ffn_out)
    (output,) = row_call(output_kernel, blocks, [middle, ffn_out], [LOW])
    qkv_own = scatter_fast(dot_left_t(inputs_one, dqkv).astype(LOW))
    gain_one_part = jnp.sum(dnormed_one_part.astype(F32) * inputs_one.astype(F32), axis=0)
    up_own = scatter_rows(grad_up)
    if is_staged:
        onehot = (blocks[None, :] == jnp.arange(count, dtype=jnp.int32)[:, None]).astype(F32)
        gain_one_part = jnp.dot(
            onehot, gain_one_part.reshape(count, -1), precision=lax.Precision.HIGHEST
        ).reshape(-1)
    small = sum_all(
        jnp.concatenate(
            [gain_one_part, gain_two_part, jnp.sum(qnorm_parts, axis=(0, 1)), jnp.sum(knorm_parts, axis=0)]
        )
    )
    own = attn_gain.shape[0]
    start = lax.axis_index(ROWS) * own
    gain_one_grad = lax.dynamic_slice_in_dim(small[:width], start, own) / attn_gain.astype(F32)
    gain_two_grad = lax.dynamic_slice_in_dim(small[width : 2 * width], start, own)
    qnorm_total = small[2 * width : 2 * width + head_dim]
    knorm_total = small[2 * width + head_dim :]
    query_grad = qkv_own[:, 2 * kcols :]
    key_grad, value_grad = unmixed(qkv_own, 0), unmixed(qkv_own, 1)
    gate_own = gate_own.astype(F32)
    down_own = down_own.astype(F32)
    up_own = up_own.astype(F32)
    (
        dnormed_one, output, gain_one_grad, query_grad, key_grad, value_grad, output_own,
        qnorm_total, knorm_total, gain_two_grad, gate_own, down_own,
    ) = tie(
        dnormed_one, output, gain_one_grad, query_grad, key_grad, value_grad, output_own,
        qnorm_total, knorm_total, gain_two_grad, gate_own, down_own,
    )
    (input_grad,) = row_call(first_back_kernel, blocks, [dnormed_one, hidden_in, dmiddle], [F32], gain_one)
    return (
        output,
        input_grad,
        gain_one_grad,
        query_grad.astype(F32),
        key_grad.astype(F32),
        value_grad.astype(F32),
        output_own.astype(F32),
        qnorm_total,
        knorm_total,
        gain_two_grad,
        gate_own,
        up_own,
        down_own,
    )


def solution(mesh):
    in_specs = (
        P(("fsdp", "context"), None),
        P("fsdp", None),
        P(("fsdp", "context"), None),
        P(("fsdp", "context")),
        P(("fsdp", "context"), "tensor"),
        P(("fsdp", "context"), "tensor"),
        P(("fsdp", "context"), "tensor"),
        P(("fsdp", "context"), "tensor"),
        P(),
        P(),
        P(("fsdp", "context")),
        P(("fsdp", "context"), "tensor"),
        P(("fsdp", "context"), "tensor"),
        P(("fsdp", "context"), "tensor"),
    )
    out_specs = (
        P(("fsdp", "context"), None),
        P(("fsdp", "context"), None),
        P(("fsdp", "context")),
        P(("fsdp", "context"), "tensor"),
        P(("fsdp", "context"), "tensor"),
        P(("fsdp", "context"), "tensor"),
        P(("fsdp", "context"), "tensor"),
        P(),
        P(),
        P(("fsdp", "context")),
        P(("fsdp", "context"), "tensor"),
        P(("fsdp", "context"), "tensor"),
        P(("fsdp", "context"), "tensor"),
    )
    return jax.shard_map(shards, mesh=mesh, in_specs=in_specs, out_specs=out_specs, check_vma=False)
```

```python
import functools

import jax
import jax.numpy as jnp
from jax import lax
from jax.experimental import pallas as pl
from jax.experimental.pallas import tpu as pltpu
from jax.sharding import PartitionSpec as P

EPS = 1e-06
THETA = 1000000.0
ROWS = ("fsdp", "context")
LOW = jnp.bfloat16
F32 = jnp.float32
LOG2E = 1.4426950408889634
VMEM_BYTES = 56 * 1024 * 1024


def dot_plain(matrix_a, matrix_b):
    return jnp.dot(matrix_a, matrix_b, preferred_element_type=F32)


def dot_right_t(matrix_a, matrix_b):
    return lax.dot_general(matrix_a, matrix_b, (((1,), (1,)), ((), ())), preferred_element_type=F32)


def dot_left_t(matrix_a, matrix_b):
    return lax.dot_general(matrix_a, matrix_b, (((0,), (0,)), ((), ())), preferred_element_type=F32)


def tie(*items):
    return lax.optimization_barrier(items)


def rms_scale(values):
    return lax.rsqrt(jnp.mean(values * values, axis=-1, keepdims=True) + EPS)


def gather_rows(shard):
    return lax.all_gather(shard, ROWS, axis=0, tiled=True)


def scatter_rows(full):
    return lax.psum_scatter(full.astype(LOW), ROWS, scatter_dimension=0, tiled=True)


def sum_tensor(partial):
    return lax.psum(partial.astype(LOW), "tensor")


def add_low(mine, other):
    return (mine.astype(F32) + other.astype(F32)).astype(LOW)


def place(index):
    return index // 4, (index // 2) % 2, index % 2


def staged_pairs(step):
    pairs = []
    for index in range(8):
        x, y, core = place(index)
        if step == "core":
            core = 1 - core
        elif step[core % len(step)] == "x":
            x = 1 - x
        else:
            y = 1 - y
        pairs.append((index, x * 4 + y * 2 + core))
    return pairs


def staged(values, step):
    return lax.ppermute(values, ROWS, staged_pairs(step))


def staged_blocks(first="xy"):
    x, y, core = place(lax.axis_index(ROWS))
    blocks = []
    for step in range(8):
        d_core, d_second, d_first = step // 4, (step // 2) % 2, step % 2
        its_core = core ^ d_core
        x_first = its_core == 0 if first == "xy" else first == "x"
        its_x = x ^ jnp.where(x_first, d_first, d_second)
        its_y = y ^ jnp.where(x_first, d_second, d_first)
        blocks.append(its_x * 4 + its_y * 2 + its_core)
    return jnp.stack(blocks).astype(jnp.int32)


OTHER = {"xy": "yx", "yx": "xy", "x": "y", "y": "x"}


def staged_pair(shard, first="xy"):
    return jnp.concatenate([shard, staged(shard, first)])


def staged_quad(pair, first="xy"):
    return jnp.concatenate([pair, staged(pair, OTHER[first])])


def staged_halves(quad):
    return [quad, staged(quad, "core")]


def staged_gather(shard):
    return jnp.concatenate(staged_halves(staged_quad(staged_pair(shard))))


def staged_scatter(full, first="xy"):
    rows = full.shape[0] // 8
    quad = add_low(full[: 4 * rows], staged(full[4 * rows :], "core"))
    pair = add_low(quad[: 2 * rows], staged(quad[2 * rows :], OTHER[first]))
    return pair[:rows].astype(F32) + staged(pair[rows:], first).astype(F32)


def sum_all(values):
    for axis in ("tensor", "context", "fsdp"):
        size = lax.axis_size(axis)
        if size & (size - 1):
            values = lax.psum(values, axis)
            continue
        bit = 1
        while bit < size:
            values = values + lax.ppermute(values, axis, [(index, index ^ bit) for index in range(size)])
            bit *= 2
    return values


def swap_context(values, bit):
    size = lax.axis_size("context")
    return lax.ppermute(values, "context", [(index, index ^ bit) for index in range(size)])


def params():
    return pltpu.CompilerParams(vmem_limit_bytes=VMEM_BYTES)


def cost(flops, moved):
    return pl.CostEstimate(flops=int(flops), bytes_accessed=int(moved), transcendentals=0)


def whole(shape):
    return pl.BlockSpec(shape, lambda *_: (0,) * len(shape))


def column(ids, step, width):
    return pl.ds(pl.multiple_of(ids[step] * width, width), width)


def stage_kernel(count, ids, values, staged_out):
    width = values.shape[1] // count
    for step in range(count):
        staged_out[:, step * width : (step + 1) * width] = values[:, column(ids, step, width)]


def by_rows(rows, body):
    def run(step, carry):
        body(pl.ds(pl.multiple_of(step * 16, 16), 16))
        return carry

    lax.fori_loop(0, rows // 16, run, 0, unroll=4)


def row_sum(parts):
    return jnp.sum(sum(parts), axis=-1, keepdims=True)


def scale_of(parts):
    size = len(parts) * parts[0].shape[1]
    return lax.rsqrt(row_sum([part * part for part in parts]) / size + EPS)


def first_norm_kernel(count, ids, hidden, gain, staged_out):
    width = hidden.shape[1] // count
    spots = [column(ids, step, width) for step in range(count)]

    def body(rows):
        parts = [hidden[rows, spot].astype(F32) for spot in spots]
        scale = scale_of(parts)
        for step in range(count):
            part = parts[step] * scale * gain[step : step + 1, :]
            staged_out[rows, step * width : (step + 1) * width] = part.astype(LOW)

    by_rows(hidden.shape[0], body)


def second_norm_kernel(count, ids, hidden, attn, gain, middle, plain_out):
    width = hidden.shape[1] // count
    spots = [column(ids, step, width) for step in range(count)]

    def body(rows):
        parts = []
        for step in range(count):
            part = attn[rows, step * width : (step + 1) * width].astype(F32)
            parts.append(hidden[rows, spots[step]].astype(F32) + part)
            middle[rows, spots[step]] = parts[step]
        scale = scale_of(parts)
        for step in range(count):
            plain_out[rows, spots[step]] = (parts[step] * scale * gain[step : step + 1, :]).astype(LOW)

    by_rows(hidden.shape[0], body)


def output_kernel(count, ids, middle, ffn, out):
    width = middle.shape[1] // count
    for step in range(count):
        spot = column(ids, step, width)
        out[:, spot] = (middle[:, spot] + ffn[:, step * width : (step + 1) * width].astype(F32)).astype(LOW)


def second_back_kernel(count, ids, grad, middle, cotangent, gain, dmiddle, staged_out, gain_out):
    width = middle.shape[1] // count

    @pl.when(pl.program_id(0) == 0)
    def _():
        gain_out[...] = jnp.zeros_like(gain_out)

    spots = [column(ids, step, width) for step in range(count)]

    def body(rows):
        parts = [middle[rows, spot] for spot in spots]
        raw = [grad[rows, spot].astype(F32) for spot in spots]
        grads = [raw[step] * gain[step : step + 1, :] for step in range(count)]
        scale = scale_of(parts)
        mean = row_sum([one * two for one, two in zip(parts, grads)]) * scale * scale / middle.shape[1]
        for step in range(count):
            term = raw[step] * parts[step] * scale
            gain_out[:, spots[step]] += term[:8] + term[8:]
            part = cotangent[rows, spots[step]].astype(F32) + scale * (grads[step] - parts[step] * mean)
            dmiddle[rows, spots[step]] = part
            staged_out[rows, step * width : (step + 1) * width] = part.astype(LOW)

    by_rows(middle.shape[0], body)


def first_back_kernel(count, ids, grad, hidden, dmiddle, gain, out):
    width = hidden.shape[1] // count
    spots = [column(ids, step, width) for step in range(count)]

    def body(rows):
        parts = [hidden[rows, spot].astype(F32) for spot in spots]
        grads = [
            grad[rows, step * width : (step + 1) * width].astype(F32) * gain[step : step + 1, :]
            for step in range(count)
        ]
        scale = scale_of(parts)
        mean = row_sum([one * two for one, two in zip(parts, grads)]) * scale * scale / hidden.shape[1]
        for step in range(count):
            out[rows, spots[step]] = dmiddle[rows, spots[step]] + scale * (grads[step] - parts[step] * mean)

    by_rows(hidden.shape[0], body)


def row_call(kernel, ids, arrays, out_types, gain=None, sums=False, after=()):
    rows, width = arrays[0].shape
    tile = min(256, rows)
    spec = pl.BlockSpec((tile, width), lambda step, *_: (step, 0))
    moved = sum(item.size * item.dtype.itemsize for item in arrays) + sum(
        rows * width * jnp.dtype(kind).itemsize for kind in out_types
    )
    gains = [] if gain is None else [gain]

    def ordered(ids, *refs):
        kernel(ids.shape[0], ids, *refs[len(after) :])

    return pl.pallas_call(
        ordered,
        grid_spec=pltpu.PrefetchScalarGridSpec(
            num_scalar_prefetch=1,
            grid=(rows // tile,),
            in_specs=[pl.BlockSpec(memory_space=pl.ANY)] * len(after)
            + [spec] * len(arrays)
            + [whole(item.shape) for item in gains],
            out_specs=[spec] * len(out_types) + [whole((8, width))] * sums,
        ),
        out_shape=[jax.ShapeDtypeStruct((rows, width), kind) for kind in out_types]
        + [jax.ShapeDtypeStruct((8, width), F32)] * sums,
        compiler_params=params(),
        cost_estimate=cost(10 * rows * width, moved),
    )(ids, *after, *arrays, *gains)


def rotate(values, cosine, sine):
    return values * cosine + pltpu.roll(values, values.shape[1] // 2, 1) * sine


def head_forward(proj, gain, cosine, sine):
    scale = rms_scale(proj)
    unit = proj * scale
    return rotate(unit * gain, cosine, sine).astype(LOW), unit, scale


def head_backward(grad, unit, scale, gain, cosine, sine):
    turned = rotate(grad.astype(LOW).astype(F32), cosine, -sine)
    scaled = turned * gain
    back = scale * (scaled - unit * jnp.mean(scaled * unit, axis=-1, keepdims=True))
    rows, width = grad.shape
    return back.astype(LOW), jnp.sum((turned * unit).reshape(rows // 8, 8, width), axis=0)


def opening_kernel(parts_in, inputs, *refs):
    weights, refs = refs[:parts_in], refs[parts_in:]
    kgain, cosine, sine, proj, qproj, out = refs
    dim = kgain.shape[1]
    kvcols, qcols = proj.shape[1], qproj.shape[1]

    def project(cols):
        total = jnp.zeros((inputs.shape[0], cols.stop - cols.start), F32)
        for step, source in enumerate(weights):
            deep = source.shape[0]
            total = total + dot_plain(inputs[:, step * deep : (step + 1) * deep], source[:, cols])
        return total

    total = project(slice(0, kvcols))
    proj[...] = total
    for head in range(kvcols // (2 * dim)):
        at = 2 * head * dim
        out[:, at : at + dim] = head_forward(total[:, at : at + dim], kgain[...], cosine[...], sine[...])[0]
        out[:, at + dim : at + 2 * dim] = total[:, at + dim : at + 2 * dim].astype(LOW)
    qproj[...] = project(slice(kvcols, kvcols + qcols))


def key_backward_kernel(mine, other, proj, gain, cosine, sine, out, norm_out):
    dim = gain.shape[1]
    total = jnp.zeros(norm_out.shape, F32)
    for head in range(proj.shape[1] // (2 * dim)):
        at = 2 * head * dim
        scale = rms_scale(proj[:, at : at + dim])
        unit = proj[:, at : at + dim] * scale
        grad = mine[:, at : at + dim].astype(F32) + other[:, at : at + dim].astype(F32)
        back, norm = head_backward(grad, unit, scale, gain[...], cosine[...], sine[...])
        total = total + norm
        out[:, at : at + dim] = back
        spot = slice(at + dim, at + 2 * dim)
        out[:, spot] = (mine[:, spot].astype(F32) + other[:, spot].astype(F32)).astype(LOW)
    norm_out[...] = total


def pair_of(info, step):
    first = info[0]
    late = step > first
    piece = jnp.where(late, 1, 0)
    key_block = jnp.where(late, step - first - 1, step)
    query_block = jnp.where(late, info[1], first)
    return piece, key_block, query_block, info[2 + key_block]


def allowed_pair(shape, half, query_block, key_block, query_seg, key_seg):
    row = lax.rem(lax.broadcasted_iota(jnp.int32, shape, 0), half)
    col = lax.broadcasted_iota(jnp.int32, shape, 1)
    return (col - row <= (query_block - key_block) * half) & (query_seg == key_seg)


def load_pieces(pieces, kv):
    rows = pieces[0].shape[0]
    for place_at, piece in enumerate(pieces):
        kv[place_at * rows : (place_at + 1) * rows, :] = piece[...]


def attend_kernel(half, count, parts_in, info, qproj, *refs):
    weights, refs = refs[:parts_in], refs[parts_in:]
    pieces, (gain, cosine, sine, seg_row, seg_col), refs = refs[:count], refs[count : count + 5], refs[count + 5 :]
    out, out_wide, log_out, part_out, qs, acc, total, segq, kv, part_sum = refs
    load_pieces(pieces, kv)
    dim = gain.shape[1]
    group = qproj.shape[1] // dim
    pairs = info.shape[0] - 1
    factor = LOG2E * dim ** (-0.5)
    for head in range(group):
        cols = slice(head * dim, (head + 1) * dim)
        query = head_forward(qproj[:, cols], gain[...], cosine[...], sine[...])[0]
        for piece in range(2):
            spot = slice(head * half, (head + 1) * half)
            rows = slice(piece * half, (piece + 1) * half)
            qs[piece, spot, :] = query[rows]
            segq[piece, spot, :] = seg_col[rows, :]
    acc[...] = jnp.zeros_like(acc)
    total[...] = jnp.zeros_like(total)
    for step in range(pairs):
        piece, key_block, query_block, spot = pair_of(info, step)
        rows = pl.ds(pl.multiple_of(spot * half, half), half)
        scores = dot_right_t(qs[piece], kv[rows, :dim])
        key_seg = seg_row[:, pl.ds(pl.multiple_of(key_block * half, half), half)]
        allowed = allowed_pair(scores.shape, half, query_block, key_block, segq[piece], key_seg)
        weight = jnp.where(allowed, jnp.exp2(scores * factor), 0.0)
        total[piece] += sum(weight[:, at : at + 128] for at in range(0, half, 128))
        acc[piece] += dot_plain(weight.astype(LOW), kv[rows, dim:])
    for piece in range(2):
        sums = jnp.sum(total[piece], axis=-1, keepdims=True)
        result = acc[piece] / sums
        logs = jnp.broadcast_to(jnp.log2(sums), result.shape)
        for head in range(group):
            cols = slice(head * dim, (head + 1) * dim)
            rows = slice(piece * half, (piece + 1) * half)
            part = result[head * half : (head + 1) * half]
            out[rows, cols] = part.astype(LOW)
            out_wide[rows, cols] = part
            log_out[rows, cols] = logs[head * half : (head + 1) * half]
    here = pl.program_id(0)

    for step, source in enumerate(weights):
        cols = slice(step * source.shape[0], (step + 1) * source.shape[0])
        term = dot_right_t(out[...], source[...])

        @pl.when(here == 0)
        def _():
            part_sum[:, cols] = term

        @pl.when(here > 0)
        def _():
            part_sum[:, cols] += term

    @pl.when(here == pl.num_programs(0) - 1)
    def _():
        part_out[...] = part_sum[...].astype(LOW)


def attend_back_kernel(half, count, info, qproj, wide, logs, grad, *refs):
    pieces, (gain, cosine, sine, seg_row, seg_col), refs = refs[:count], refs[count : count + 5], refs[count + 5 :]
    dq_out, keep_out, send_out, norm_out, qs, gs, segq, ls, ds, dq, dkv, kv = refs
    load_pieces(pieces, kv)
    dim = gain.shape[1]
    group = qproj.shape[1] // dim
    pairs = info.shape[0] - 1
    plain = dim ** (-0.5)
    factor = LOG2E * plain
    for head in range(group):
        cols = slice(head * dim, (head + 1) * dim)
        query = head_forward(qproj[:, cols], gain[...], cosine[...], sine[...])[0]
        delta = jnp.sum(grad[:, cols].astype(F32) * wide[:, cols], axis=-1, keepdims=True)
        for piece in range(2):
            spot = slice(head * half, (head + 1) * half)
            rows = slice(piece * half, (piece + 1) * half)
            qs[piece, spot, :] = query[rows]
            gs[piece, spot, :] = grad[rows, cols]
            segq[piece, spot, :] = seg_col[rows, :]
            ls[piece, spot, :] = logs[rows, head * dim : head * dim + 1]
            ds[piece, spot, :] = delta[rows]
    dq[...] = jnp.zeros_like(dq)
    dkv[...] = jnp.zeros_like(dkv)
    for step in range(pairs):
        piece, key_block, query_block, spot = pair_of(info, step)
        rows = pl.ds(pl.multiple_of(spot * half, half), half)
        query, outer = qs[piece], gs[piece]
        scores = dot_right_t(query, kv[rows, :dim])
        key_seg = seg_row[:, pl.ds(pl.multiple_of(key_block * half, half), half)]
        allowed = allowed_pair(scores.shape, half, query_block, key_block, segq[piece], key_seg)
        prob = jnp.where(allowed, jnp.exp2(scores * factor - ls[piece]), 0.0)
        dprob = dot_right_t(outer, kv[rows, dim:])
        dscores = (prob * (dprob - ds[piece])).astype(LOW)
        dq[piece] += dot_plain(dscores, kv[rows, :dim])
        dkv[rows, :dim] += dot_left_t(dscores, query)
        dkv[rows, dim:] += dot_left_t(prob.astype(LOW), outer)
    rows = 2 * half
    for at in range(count):
        target = send_out if at % 2 else keep_out
        spot, low = slice(at // 2 * rows, (at // 2 + 1) * rows), slice(at * rows, (at + 1) * rows)
        target[spot, :dim] = (dkv[low, :dim] * plain).astype(LOW)
        target[spot, dim:] = dkv[low, dim:].astype(LOW)
    total = jnp.zeros(norm_out.shape[1:], F32)
    for head in range(group):
        cols = slice(head * dim, (head + 1) * dim)
        scale = rms_scale(qproj[:, cols])
        unit = qproj[:, cols] * scale
        grads = jnp.concatenate([dq[piece, head * half : (head + 1) * half, :] for piece in range(2)]) * plain
        back, norm = head_backward(grads, unit, scale, gain[...], cosine[...], sine[...])
        total = total + norm
        dq_out[:, cols] = back
    norm_out[0] = total


def heads_spec(rows, width):
    return pl.BlockSpec((rows, width), lambda head, *_: (0, head))


def attend(info, qproj, weights, pieces, gain, cosine, sine, seg_row, seg_col):
    rows, qcols = qproj.shape
    count, kvcols = len(pieces), pieces[0].shape[1]
    dim = gain.shape[1]
    heads = kvcols // (2 * dim)
    wide = qcols // heads
    half = rows // 2
    stacked = half * (wide // dim)
    qspec, kspec = heads_spec(rows, wide), heads_spec(rows, 2 * dim)
    tables = (gain, cosine, sine, seg_row, seg_col)
    width = sum(item.shape[0] for item in weights)
    return pl.pallas_call(
        functools.partial(attend_kernel, half, count, len(weights)),
        grid_spec=pltpu.PrefetchScalarGridSpec(
            num_scalar_prefetch=1,
            grid=(heads,),
            in_specs=[qspec]
            + [heads_spec(item.shape[0], wide) for item in weights]
            + [kspec] * count
            + [whole(item.shape) for item in tables],
            out_specs=[qspec] * 3 + [whole((rows, width))],
            scratch_shapes=[
                pltpu.VMEM((2, stacked, dim), LOW),
                pltpu.VMEM((2, stacked, dim), F32),
                pltpu.VMEM((2, stacked, 128), F32),
                pltpu.VMEM((2, stacked, 1), jnp.int32),
                pltpu.VMEM((count * rows, 2 * dim), LOW),
                pltpu.VMEM((rows, width), F32),
            ],
        ),
        out_shape=[jax.ShapeDtypeStruct((rows, qcols), kind) for kind in (LOW, F32, F32)]
        + [jax.ShapeDtypeStruct((rows, width), LOW)],
        compiler_params=params(),
        cost_estimate=cost(2 * rows * count * rows * qcols * 2, 8 * rows * qcols * 2),
    )(info, qproj, *weights, *pieces, *tables)


def attend_back(info, qproj, wide_out, logs, grad, pieces, gain, cosine, sine, seg_row, seg_col):
    rows, qcols = qproj.shape
    count, kvcols = len(pieces), pieces[0].shape[1]
    dim = gain.shape[1]
    heads = kvcols // (2 * dim)
    wide = qcols // heads
    half = rows // 2
    stacked = half * (wide // dim)
    qspec, kspec = heads_spec(rows, wide), heads_spec(rows, 2 * dim)
    part = heads_spec(count // 2 * rows, 2 * dim)
    tables = (gain, cosine, sine, seg_row, seg_col)
    return pl.pallas_call(
        functools.partial(attend_back_kernel, half, count),
        grid_spec=pltpu.PrefetchScalarGridSpec(
            num_scalar_prefetch=1,
            grid=(heads,),
            in_specs=[qspec] * 4 + [kspec] * count + [whole(item.shape) for item in tables],
            out_specs=[qspec, part, part, pl.BlockSpec((1, 8, dim), lambda head, *_: (head, 0, 0))],
            scratch_shapes=[
                pltpu.VMEM((2, stacked, dim), LOW),
                pltpu.VMEM((2, stacked, dim), LOW),
                pltpu.VMEM((2, stacked, 1), jnp.int32),
                pltpu.VMEM((2, stacked, 1), F32),
                pltpu.VMEM((2, stacked, 1), F32),
                pltpu.VMEM((2, stacked, dim), F32),
                pltpu.VMEM((count * rows, 2 * dim), F32),
                pltpu.VMEM((count * rows, 2 * dim), LOW),
            ],
        ),
        out_shape=[
            jax.ShapeDtypeStruct((rows, qcols), LOW),
            jax.ShapeDtypeStruct((count // 2 * rows, kvcols), LOW),
            jax.ShapeDtypeStruct((count // 2 * rows, kvcols), LOW),
            jax.ShapeDtypeStruct((heads, 8, dim), F32),
        ],
        compiler_params=params(),
        cost_estimate=cost(0, rows * qcols),
    )(info, qproj, wide_out, logs, grad, *pieces, *tables)


def assemble_kernel(dim, key, value, query, out):
    kcols = key.shape[1]
    for head in range(kcols // dim):
        spot = slice(head * dim, (head + 1) * dim)
        out[:, 2 * head * dim : (2 * head + 1) * dim] = key[:, spot]
        out[:, (2 * head + 1) * dim : (2 * head + 2) * dim] = value[:, spot]
    out[:, 2 * kcols :] = query[...]


def assemble(key, value, query, dim):
    cols = 2 * key.shape[1] + query.shape[1]
    return pl.pallas_call(
        functools.partial(assemble_kernel, dim),
        out_shape=jax.ShapeDtypeStruct((key.shape[0], cols), LOW),
        compiler_params=params(),
        cost_estimate=cost(0, 4 * key.shape[0] * cols),
    )(key, value, query)


def opening(inputs, halves, kvcols, qcols, kgain, cosine, sine):
    rows, width = inputs.shape
    tile = min(256, rows)
    shapes = [(kvcols, F32), (qcols, F32), (kvcols, LOW)]

    def tiled(cols):
        return pl.BlockSpec((tile, cols), lambda step: (step, 0))

    return pl.pallas_call(
        functools.partial(opening_kernel, len(halves)),
        grid=(rows // tile,),
        in_specs=[tiled(width)]
        + [whole(item.shape) for item in halves]
        + [whole(kgain.shape), tiled(cosine.shape[1]), tiled(sine.shape[1])],
        out_specs=[tiled(cols) for cols, _ in shapes],
        out_shape=[jax.ShapeDtypeStruct((rows, cols), kind) for cols, kind in shapes],
        compiler_params=params(),
        cost_estimate=cost(2 * rows * width * (kvcols + qcols), 4 * rows * width + 2 * width * kvcols),
    )(inputs, *halves, kgain, cosine, sine)


def key_backward(mine, other, proj, gain, cosine, sine):
    return pl.pallas_call(
        key_backward_kernel,
        out_shape=[
            jax.ShapeDtypeStruct(proj.shape, LOW),
            jax.ShapeDtypeStruct((8, gain.shape[1]), F32),
        ],
        compiler_params=params(),
        cost_estimate=cost(0, proj.size),
    )(mine, other, proj, gain, cosine, sine)


def feed_kernel(inputs, gate, up, dproduct, product, dgate, dup, dinputs, total):
    step = pl.program_id(0)
    gate_in = dot_plain(inputs[...], gate[...])
    up_in = dot_plain(inputs[...], up[...])
    sigmoid = 1.0 / (1.0 + jnp.exp(-gate_in))
    active = gate_in * sigmoid
    product[...] = (active * up_in).astype(LOW)
    grad = dproduct[...]
    dgate_low = (grad * up_in * sigmoid * (1.0 + gate_in * (1.0 - sigmoid))).astype(LOW)
    dup_low = (grad * active).astype(LOW)
    dgate[...] = dgate_low
    dup[...] = dup_low
    part = dot_right_t(dgate_low, gate[...]) + dot_right_t(dup_low, up[...])

    @pl.when(step == 0)
    def _():
        total[...] = part

    @pl.when(step > 0)
    def _():
        total[...] += part

    @pl.when(step == pl.num_programs(0) - 1)
    def _():
        dinputs[...] = total[...].astype(LOW)


def feed(inputs, gate_up, dproduct):
    rows, width = inputs.shape
    units = dproduct.shape[1]
    tile = min(256, units)
    count = units // tile
    gspec = pl.BlockSpec((width, tile), lambda step: (0, step))
    uspec = pl.BlockSpec((width, tile), lambda step: (0, step + count))
    tspec = pl.BlockSpec((rows, tile), lambda step: (0, step))
    return pl.pallas_call(
        feed_kernel,
        grid=(count,),
        in_specs=[whole((rows, width)), gspec, uspec, tspec],
        out_specs=[tspec, tspec, tspec, whole((rows, width))],
        out_shape=[jax.ShapeDtypeStruct((rows, units), LOW)] * 3 + [jax.ShapeDtypeStruct((rows, width), LOW)],
        scratch_shapes=[pltpu.VMEM((rows, width), F32)],
        compiler_params=params(),
        cost_estimate=cost(8 * rows * width * units, 4 * width * units + 10 * rows * units),
    )(inputs, gate_up, gate_up, dproduct)


def shards(
    hidden_in,
    segments,
    cotangent,
    attn_gain,
    query_weight,
    key_weight,
    value_weight,
    output_weight,
    qnorm_gain,
    knorm_gain,
    ffn_gain,
    gate_weight,
    up_weight,
    down_weight,
):
    is_staged = lax.axis_size("fsdp") == 2 and lax.axis_size("context") == 4
    gather_fast = staged_gather if is_staged else gather_rows
    scatter_fast = staged_scatter if is_staged else scatter_rows
    head_dim = qnorm_gain.shape[0]
    local_rows, width = hidden_in.shape
    shard_rows = query_weight.shape[0]
    pieces = lax.axis_size("context")
    total_rows = local_rows * pieces
    half_rows = local_rows // 2
    value_heads = key_weight.shape[1] // head_dim
    qcols = query_weight.shape[1]
    kcols = key_weight.shape[1]

    def unmixed(both, which):
        starts = [(2 * head + which) * head_dim for head in range(value_heads)]
        return jnp.concatenate([both[:, at : at + head_dim] for at in starts], axis=1)

    blocks = staged_blocks() if is_staged else jnp.zeros((1,), jnp.int32)
    count = blocks.shape[0]
    near_shard = assemble(key_weight, value_weight, query_weight, head_dim)
    gains = gather_fast(jnp.stack([attn_gain, ffn_gain])).reshape(-1, 2, shard_rows).astype(F32)
    gain_one = gains[:, 0].reshape(count, -1)
    gain_two = gains[:, 1].reshape(count, -1)

    me = lax.axis_index("context")
    last = 2 * pieces - 1
    spots = []
    for block in range(2 * pieces):
        owner = block if block < pieces else last - block
        spots.append(2 * (owner ^ me) + (0 if block < pieces else 1))
    info = jnp.stack([me, last - me] + spots).astype(jnp.int32)
    ramp = jnp.arange(half_rows, dtype=jnp.int32)
    positions = jnp.concatenate([me * half_rows + ramp, (last - me) * half_rows + ramp])
    seg_col = jnp.concatenate(
        [
            lax.dynamic_slice_in_dim(segments[0], block * half_rows, half_rows)
            for block in (me, last - me)
        ]
    )[:, None]
    half_dim = head_dim // 2
    inverse = THETA ** (-(jnp.arange(half_dim).astype(F32) * 2.0 / head_dim))
    angles = positions.astype(F32)[:, None] * inverse[None, :]
    cosine = jnp.cos(angles)
    sine = jnp.sin(angles)
    cosine = jnp.concatenate([cosine, cosine], axis=1)
    sine = jnp.concatenate([-sine, sine], axis=1)
    qgain = qnorm_gain.astype(F32)[None, :]
    kgain = knorm_gain.astype(F32)[None, :]

    (cot_staged,) = row_call(stage_kernel, blocks, [cotangent], [LOW])
    out_blocks = staged_blocks("y") if is_staged else blocks
    if is_staged:
        match = (out_blocks[:, None] == blocks[None, :]).astype(F32)
        gain_two = jnp.dot(match, gain_two, precision=lax.Precision.HIGHEST)
    if is_staged:
        near_pair = staged_pair(near_shard)
        near_far = staged(near_pair, "yx")
        near_far, gain_one, gain_two, blocks, info, seg_col, cosine, sine = tie(
            near_far, gain_one, gain_two, blocks, info, seg_col, cosine, sine
        )
        near_last, out_shard = tie(staged(near_far, "core"), output_weight)
        near_halves = [near_pair, near_far, staged(near_pair, "core"), near_last]
        out_pair = staged_pair(out_shard, "y")
    else:
        near_halves = [gather_rows(near_shard)]
    (inputs_one,) = row_call(first_norm_kernel, blocks, [hidden_in], [LOW], gain_one)
    kv_proj, query_proj, kv_own = opening(inputs_one, near_halves, 2 * kcols, qcols, kgain, cosine, sine)
    if is_staged:
        out_pair, kv_own = tie(out_pair, kv_own)
        out_halves = staged_halves(staged_quad(out_pair, "y"))
    else:
        out_halves = [gather_rows(output_weight)]
    kv_across = swap_context(kv_own, 2)
    kv_pieces = [kv_own, swap_context(kv_own, 1), kv_across, swap_context(kv_across, 1)]
    gate_up_shard, kv_proj = tie(jnp.concatenate([gate_weight, up_weight], axis=1), kv_proj)
    gate_up = gather_rows(gate_up_shard)
    attended, attended_wide, logs, attn_part = attend(
        info, query_proj, out_halves, kv_pieces, qgain, cosine, sine, segments, seg_col
    )
    down_shard, logs = tie(down_weight, logs)
    down_full = gather_fast(down_shard)
    attn_out = sum_tensor(attn_part)
    dproduct = dot_plain(cot_staged, down_full)
    near_full = jnp.concatenate(near_halves)
    out_full = jnp.concatenate(out_halves)
    attn_out, dproduct, near_full, out_full = tie(attn_out, dproduct, near_full, out_full)
    middle, inputs_two = row_call(second_norm_kernel, out_blocks, [hidden_in, attn_out], [F32, LOW], gain_two)
    product, dgate, dup_low, dnormed_two_part = feed(inputs_two, gate_up, dproduct)
    dnormed_two = sum_tensor(dnormed_two_part)

    ffn_part = dot_right_t(product, down_full).astype(LOW)
    down_own = scatter_rows(dot_left_t(cotangent, product))
    grad_gate = dot_left_t(inputs_two, dgate).astype(LOW)
    grad_up = dot_left_t(inputs_two, dup_low).astype(LOW)
    dnormed_two, ffn_part, grad_gate, grad_up = tie(dnormed_two, ffn_part, grad_gate, grad_up)
    ffn_out = sum_tensor(ffn_part)
    dmiddle, dattn, gain_two_sums = row_call(
        second_back_kernel, out_blocks, [dnormed_two, middle, cotangent], [F32, LOW], gain_two, True
    )
    gain_two_part = jnp.sum(gain_two_sums, axis=0) / lax.axis_size("tensor")
    dattended = dot_plain(dattn, out_full).astype(LOW)
    dquery, dkv_keep, dkv_send, qnorm_parts = attend_back(
        info, query_proj, attended_wide, logs, dattended, kv_pieces, qgain, cosine, sine, segments, seg_col
    )
    grad_gate, down_own, qnorm_parts = tie(grad_gate, down_own, qnorm_parts)
    gate_own = scatter_rows(grad_gate)
    dkv_pair = add_low(dkv_keep, swap_context(dkv_send, 1))
    dkv, knorm_parts = key_backward(
        dkv_pair[:local_rows], swap_context(dkv_pair[local_rows:], 2), kv_proj, kgain, cosine, sine
    )
    grad_output = dot_left_t(dattn, attended).astype(LOW)
    output_own = staged_scatter(grad_output, "y") if is_staged else scatter_rows(grad_output)
    dqkv = jnp.concatenate([dkv, dquery], axis=1)
    dnormed_one_part = dot_right_t(dqkv, near_full).astype(LOW)
    later_part, ffn_out = tie(dnormed_one_part, ffn_out)
    dnormed_one = sum_tensor(later_part)
    grad_up, gate_own, ffn_out = tie(grad_up, gate_own, ffn_out)
    (output,) = row_call(output_kernel, blocks, [middle, ffn_out], [LOW])
    qkv_own = scatter_fast(dot_left_t(inputs_one, dqkv).astype(LOW))
    gain_one_part = jnp.sum(dnormed_one_part.astype(F32) * inputs_one.astype(F32), axis=0)
    up_own = scatter_rows(grad_up)
    if is_staged:
        onehot = (blocks[None, :] == jnp.arange(count, dtype=jnp.int32)[:, None]).astype(F32)
        gain_one_part = jnp.dot(
            onehot, gain_one_part.reshape(count, -1), precision=lax.Precision.HIGHEST
        ).reshape(-1)
    small = sum_all(
        jnp.concatenate(
            [gain_one_part, gain_two_part, jnp.sum(qnorm_parts, axis=(0, 1)), jnp.sum(knorm_parts, axis=0)]
        )
    )
    own = attn_gain.shape[0]
    start = lax.axis_index(ROWS) * own
    gain_one_grad = lax.dynamic_slice_in_dim(small[:width], start, own) / attn_gain.astype(F32)
    gain_two_grad = lax.dynamic_slice_in_dim(small[width : 2 * width], start, own)
    qnorm_total = small[2 * width : 2 * width + head_dim]
    knorm_total = small[2 * width + head_dim :]
    qkv_own = qkv_own.astype(F32)
    query_grad = qkv_own[:, 2 * kcols :]
    key_grad, value_grad = unmixed(qkv_own, 0), unmixed(qkv_own, 1)
    output_own = output_own.astype(F32)
    gate_own = gate_own.astype(F32)
    down_own = down_own.astype(F32)
    done = [output, small, query_grad, key_grad, value_grad, output_own, gate_own, down_own]
    (input_grad,) = row_call(
        first_back_kernel, blocks, [dnormed_one, hidden_in, dmiddle], [F32], gain_one, after=done
    )
    return (
        output,
        input_grad,
        gain_one_grad,
        query_grad,
        key_grad,
        value_grad,
        output_own,
        qnorm_total,
        knorm_total,
        gain_two_grad,
        gate_own,
        up_own.astype(F32),
        down_own,
    )


def solution(mesh):
    in_specs = (
        P(("fsdp", "context"), None),
        P("fsdp", None),
        P(("fsdp", "context"), None),
        P(("fsdp", "context")),
        P(("fsdp", "context"), "tensor"),
        P(("fsdp", "context"), "tensor"),
        P(("fsdp", "context"), "tensor"),
        P(("fsdp", "context"), "tensor"),
        P(),
        P(),
        P(("fsdp", "context")),
        P(("fsdp", "context"), "tensor"),
        P(("fsdp", "context"), "tensor"),
        P(("fsdp", "context"), "tensor"),
    )
    out_specs = (
        P(("fsdp", "context"), None),
        P(("fsdp", "context"), None),
        P(("fsdp", "context")),
        P(("fsdp", "context"), "tensor"),
        P(("fsdp", "context"), "tensor"),
        P(("fsdp", "context"), "tensor"),
        P(("fsdp", "context"), "tensor"),
        P(),
        P(),
        P(("fsdp", "context")),
        P(("fsdp", "context"), "tensor"),
        P(("fsdp", "context"), "tensor"),
        P(("fsdp", "context"), "tensor"),
    )
    return jax.shard_map(shards, mesh=mesh, in_specs=in_specs, out_specs=out_specs, check_vma=False)
```

```python
import functools

import jax
import jax.numpy as jnp
from jax import lax
from jax.experimental import pallas as pl
from jax.experimental.pallas import tpu as pltpu
from jax.sharding import PartitionSpec as P

EPS = 1e-06
THETA = 1000000.0
ROWS = ("fsdp", "context")
LOW = jnp.bfloat16
F32 = jnp.float32
LOG2E = 1.4426950408889634
VMEM_MIB = 56


def dot_plain(matrix_a, matrix_b):
    return jnp.dot(matrix_a, matrix_b, preferred_element_type=F32)


def dot_right_t(matrix_a, matrix_b):
    return lax.dot_general(matrix_a, matrix_b, (((1,), (1,)), ((), ())), preferred_element_type=F32)


def dot_left_t(matrix_a, matrix_b):
    return lax.dot_general(matrix_a, matrix_b, (((0,), (0,)), ((), ())), preferred_element_type=F32)


def tie(*items):
    return lax.optimization_barrier(items)


def rms_scale(values):
    return lax.rsqrt(jnp.mean(values * values, axis=-1, keepdims=True) + EPS)


def gather_rows(shard):
    return lax.all_gather(shard, ROWS, axis=0, tiled=True)


def scatter_rows(full):
    return lax.psum_scatter(full.astype(LOW), ROWS, scatter_dimension=0, tiled=True)


def sum_tensor(partial):
    return lax.psum(partial.astype(LOW), "tensor")


def add_low(mine, other):
    return (mine.astype(F32) + other.astype(F32)).astype(LOW)


def place(index):
    return index // 4, (index // 2) % 2, index % 2


def staged_pairs(step):
    pairs = []
    for index in range(8):
        x, y, core = place(index)
        if step == "core":
            core = 1 - core
        elif step[core % len(step)] == "x":
            x = 1 - x
        else:
            y = 1 - y
        pairs.append((index, x * 4 + y * 2 + core))
    return pairs


def staged(values, step):
    return lax.ppermute(values, ROWS, staged_pairs(step))


def staged_blocks(first="xy"):
    x, y, core = place(lax.axis_index(ROWS))
    blocks = []
    for step in range(8):
        d_core, d_second, d_first = step // 4, (step // 2) % 2, step % 2
        its_core = core ^ d_core
        x_first = its_core == 0 if first == "xy" else first == "x"
        its_x = x ^ jnp.where(x_first, d_first, d_second)
        its_y = y ^ jnp.where(x_first, d_second, d_first)
        blocks.append(its_x * 4 + its_y * 2 + its_core)
    return jnp.stack(blocks).astype(jnp.int32)


OTHER = {"xy": "yx", "yx": "xy", "x": "y", "y": "x"}


def staged_pair(shard, first="xy"):
    return jnp.concatenate([shard, staged(shard, first)])


def staged_quad(pair, first="xy"):
    return jnp.concatenate([pair, staged(pair, OTHER[first])])


def staged_halves(quad):
    return [quad, staged(quad, "core")]


def staged_gather(shard):
    return jnp.concatenate(staged_halves(staged_quad(staged_pair(shard))))


def staged_scatter(full, first="xy"):
    rows = full.shape[0] // 8
    quad = add_low(full[: 4 * rows], staged(full[4 * rows :], "core"))
    pair = add_low(quad[: 2 * rows], staged(quad[2 * rows :], OTHER[first]))
    return pair[:rows].astype(F32) + staged(pair[rows:], first).astype(F32)


def sum_all(values):
    for axis in ("tensor", "context", "fsdp"):
        size = lax.axis_size(axis)
        if size & (size - 1):
            values = lax.psum(values, axis)
            continue
        bit = 1
        while bit < size:
            values = values + lax.ppermute(values, axis, [(index, index ^ bit) for index in range(size)])
            bit *= 2
    return values


def swap_context(values, bit):
    size = lax.axis_size("context")
    return lax.ppermute(values, "context", [(index, index ^ bit) for index in range(size)])


def params(mib=VMEM_MIB):
    return pltpu.CompilerParams(vmem_limit_bytes=mib * 1024 * 1024)


def cost(flops, moved):
    return pl.CostEstimate(flops=int(flops), bytes_accessed=int(moved), transcendentals=0)


def whole(shape):
    return pl.BlockSpec(shape, lambda *_: (0,) * len(shape))


def column(ids, step, width):
    return pl.ds(pl.multiple_of(ids[step] * width, width), width)


def stage_kernel(count, ids, values, staged_out):
    width = values.shape[1] // count
    for step in range(count):
        staged_out[:, step * width : (step + 1) * width] = values[:, column(ids, step, width)]


def by_rows(rows, body):
    def run(step, carry):
        body(pl.ds(pl.multiple_of(step * 16, 16), 16))
        return carry

    lax.fori_loop(0, rows // 16, run, 0, unroll=4)


def row_sum(parts):
    return jnp.sum(sum(parts), axis=-1, keepdims=True)


def scale_of(parts):
    size = len(parts) * parts[0].shape[1]
    return lax.rsqrt(row_sum([part * part for part in parts]) / size + EPS)


def first_norm_kernel(count, ids, hidden, gain, staged_out):
    width = hidden.shape[1] // count
    spots = [column(ids, step, width) for step in range(count)]

    def body(rows):
        parts = [hidden[rows, spot].astype(F32) for spot in spots]
        scale = scale_of(parts)
        for step in range(count):
            part = parts[step] * scale * gain[step : step + 1, :]
            staged_out[rows, step * width : (step + 1) * width] = part.astype(LOW)

    by_rows(hidden.shape[0], body)


def second_norm_kernel(count, ids, hidden, attn, gain, middle, plain_out):
    width = hidden.shape[1] // count
    spots = [column(ids, step, width) for step in range(count)]

    def body(rows):
        parts = []
        for step in range(count):
            part = attn[rows, step * width : (step + 1) * width].astype(F32)
            parts.append(hidden[rows, spots[step]].astype(F32) + part)
            middle[rows, spots[step]] = parts[step]
        scale = scale_of(parts)
        for step in range(count):
            plain_out[rows, spots[step]] = (parts[step] * scale * gain[step : step + 1, :]).astype(LOW)

    by_rows(hidden.shape[0], body)


def output_kernel(count, ids, middle, ffn, out):
    width = middle.shape[1] // count
    for step in range(count):
        spot = column(ids, step, width)
        out[:, spot] = (middle[:, spot] + ffn[:, step * width : (step + 1) * width].astype(F32)).astype(LOW)


def second_back_kernel(count, ids, grad, middle, cotangent, gain, dmiddle, staged_out, gain_out):
    width = middle.shape[1] // count

    @pl.when(pl.program_id(0) == 0)
    def _():
        gain_out[...] = jnp.zeros_like(gain_out)

    spots = [column(ids, step, width) for step in range(count)]

    def body(rows):
        parts = [middle[rows, spot] for spot in spots]
        raw = [grad[rows, spot].astype(F32) for spot in spots]
        grads = [raw[step] * gain[step : step + 1, :] for step in range(count)]
        scale = scale_of(parts)
        mean = row_sum([one * two for one, two in zip(parts, grads)]) * scale * scale / middle.shape[1]
        for step in range(count):
            term = raw[step] * parts[step] * scale
            gain_out[:, spots[step]] += term[:8] + term[8:]
            part = cotangent[rows, spots[step]].astype(F32) + scale * (grads[step] - parts[step] * mean)
            dmiddle[rows, spots[step]] = part
            staged_out[rows, step * width : (step + 1) * width] = part.astype(LOW)

    by_rows(middle.shape[0], body)


def first_back_kernel(count, ids, grad, hidden, dmiddle, gain, out):
    width = hidden.shape[1] // count
    spots = [column(ids, step, width) for step in range(count)]

    def body(rows):
        parts = [hidden[rows, spot].astype(F32) for spot in spots]
        grads = [
            grad[rows, step * width : (step + 1) * width].astype(F32) * gain[step : step + 1, :]
            for step in range(count)
        ]
        scale = scale_of(parts)
        mean = row_sum([one * two for one, two in zip(parts, grads)]) * scale * scale / hidden.shape[1]
        for step in range(count):
            out[rows, spots[step]] = dmiddle[rows, spots[step]] + scale * (grads[step] - parts[step] * mean)

    by_rows(hidden.shape[0], body)


def row_call(kernel, ids, arrays, out_types, gain=None, after=(), sums=False, mib=VMEM_MIB):
    rows, width = arrays[0].shape
    tile = min(256, rows)
    spec = pl.BlockSpec((tile, width), lambda step, *_: (step, 0))
    moved = sum(item.size * item.dtype.itemsize for item in arrays) + sum(
        rows * width * jnp.dtype(kind).itemsize for kind in out_types
    )
    gains = [] if gain is None else [gain]

    def ordered(ids, *refs):
        kernel(ids.shape[0], ids, *refs[len(after) :])

    return pl.pallas_call(
        ordered,
        grid_spec=pltpu.PrefetchScalarGridSpec(
            num_scalar_prefetch=1,
            grid=(rows // tile,),
            in_specs=[pl.BlockSpec(memory_space=pl.ANY)] * len(after)
            + [spec] * len(arrays)
            + [whole(item.shape) for item in gains],
            out_specs=[spec] * len(out_types) + [whole((8, width))] * sums,
        ),
        out_shape=[jax.ShapeDtypeStruct((rows, width), kind) for kind in out_types]
        + [jax.ShapeDtypeStruct((8, width), F32)] * sums,
        compiler_params=params(mib),
        cost_estimate=cost(10 * rows * width, moved),
    )(ids, *after, *arrays, *gains)


def rotate(values, cosine, sine):
    return values * cosine + pltpu.roll(values, values.shape[1] // 2, 1) * sine


def head_forward(proj, gain, cosine, sine):
    scale = rms_scale(proj)
    unit = proj * scale
    return rotate(unit * gain, cosine, sine).astype(LOW), unit, scale


def head_backward(grad, unit, scale, gain, cosine, sine):
    turned = rotate(grad.astype(LOW).astype(F32), cosine, -sine)
    scaled = turned * gain
    back = scale * (scaled - unit * jnp.mean(scaled * unit, axis=-1, keepdims=True))
    rows, width = grad.shape
    return back.astype(LOW), jnp.sum((turned * unit).reshape(rows // 8, 8, width), axis=0)


def opening_kernel(parts_in, inputs, *refs):
    weights, refs = refs[:parts_in], refs[parts_in:]
    kgain, cosine, sine, proj, qproj, out = refs
    dim = kgain.shape[1]
    kvcols, qcols = proj.shape[1], qproj.shape[1]

    def project(cols):
        total = jnp.zeros((inputs.shape[0], cols.stop - cols.start), F32)
        for step, source in enumerate(weights):
            deep = source.shape[0]
            total = total + dot_plain(inputs[:, step * deep : (step + 1) * deep], source[:, cols])
        return total

    total = project(slice(0, kvcols))
    proj[...] = total
    for head in range(kvcols // (2 * dim)):
        at = 2 * head * dim
        out[:, at : at + dim] = head_forward(total[:, at : at + dim], kgain[...], cosine[...], sine[...])[0]
        out[:, at + dim : at + 2 * dim] = total[:, at + dim : at + 2 * dim].astype(LOW)
    qproj[...] = project(slice(kvcols, kvcols + qcols))


def key_backward_kernel(mine, other, proj, gain, cosine, sine, out, norm_out):
    dim = gain.shape[1]
    total = jnp.zeros(norm_out.shape, F32)
    for head in range(proj.shape[1] // (2 * dim)):
        at = 2 * head * dim
        scale = rms_scale(proj[:, at : at + dim])
        unit = proj[:, at : at + dim] * scale
        grad = mine[:, at : at + dim].astype(F32) + other[:, at : at + dim].astype(F32)
        back, norm = head_backward(grad, unit, scale, gain[...], cosine[...], sine[...])
        total = total + norm
        out[:, at : at + dim] = back
        spot = slice(at + dim, at + 2 * dim)
        out[:, spot] = (mine[:, spot].astype(F32) + other[:, spot].astype(F32)).astype(LOW)
    norm_out[...] = total


def pair_of(info, step):
    first = info[0]
    late = step > first
    piece = jnp.where(late, 1, 0)
    key_block = jnp.where(late, step - first - 1, step)
    query_block = jnp.where(late, info[1], first)
    return piece, key_block, query_block, info[2 + key_block]


def allowed_pair(shape, half, query_block, key_block, query_seg, key_seg):
    row = lax.rem(lax.broadcasted_iota(jnp.int32, shape, 0), half)
    col = lax.broadcasted_iota(jnp.int32, shape, 1)
    return (col - row <= (query_block - key_block) * half) & (query_seg == key_seg)


def load_pieces(pieces, kv):
    rows = pieces[0].shape[0]
    for place_at, piece in enumerate(pieces):
        kv[place_at * rows : (place_at + 1) * rows, :] = piece[...]


def attend_kernel(half, count, parts_in, info, qproj, *refs):
    weights, refs = refs[:parts_in], refs[parts_in:]
    pieces, (gain, cosine, sine, seg_row, seg_col), refs = refs[:count], refs[count : count + 5], refs[count + 5 :]
    out, out_wide, log_out, part_out, qs, acc, total, segq, kv = refs
    load_pieces(pieces, kv)
    dim = gain.shape[1]
    heads = kv.shape[1] // (2 * dim)
    group = qproj.shape[1] // (dim * heads)
    pairs = info.shape[0] - 1
    factor = LOG2E * dim ** (-0.5)
    for piece in range(2):
        for member in range(group):
            segq[piece, member * half : (member + 1) * half, :] = seg_col[piece * half : (piece + 1) * half, :1]
    for head in range(heads):
        for member in range(group):
            at = (head * group + member) * dim
            query = head_forward(qproj[:, at : at + dim], gain[...], cosine[...], sine[...])[0]
            for piece in range(2):
                qs[head, piece, member * half : (member + 1) * half, :] = query[piece * half : (piece + 1) * half]
    acc[...] = jnp.zeros_like(acc)
    total[...] = jnp.zeros_like(total)
    for step in range(pairs):
        piece, key_block, query_block, spot = pair_of(info, step)
        rows = pl.ds(pl.multiple_of(spot * half, half), half)
        key_seg = seg_row[:, pl.ds(pl.multiple_of(key_block * half, half), half)]
        allowed = allowed_pair((group * half, half), half, query_block, key_block, segq[piece], key_seg)
        for head in range(heads):
            at = 2 * head * dim
            scores = dot_right_t(qs[head, piece], kv[rows, at : at + dim])
            weight = jnp.where(allowed, jnp.exp2(scores * factor), 0.0)
            total[head, piece] += sum(weight[:, col : col + 128] for col in range(0, half, 128))
            acc[head, piece] += dot_plain(weight.astype(LOW), kv[rows, at + dim : at + 2 * dim])
    for head in range(heads):
        for piece in range(2):
            sums = jnp.sum(total[head, piece], axis=-1, keepdims=True)
            result = acc[head, piece] / sums
            logs = jnp.broadcast_to(jnp.log2(sums), result.shape)
            rows = slice(piece * half, (piece + 1) * half)
            for member in range(group):
                at = (head * group + member) * dim
                part = result[member * half : (member + 1) * half]
                out[rows, at : at + dim] = part.astype(LOW)
                out_wide[rows, at : at + dim] = part
                log_out[rows, at : at + dim] = logs[member * half : (member + 1) * half]
    for step, source in enumerate(weights):
        cols = slice(step * source.shape[0], (step + 1) * source.shape[0])
        part_out[:, cols] = dot_right_t(out[...], source[...]).astype(LOW)


def attend_back_kernel(half, count, info, qproj, wide, logs, grad, *refs):
    pieces, (gain, cosine, sine, seg_row, seg_col), refs = refs[:count], refs[count : count + 5], refs[count + 5 :]
    dq_out, keep_out, send_out, norm_out, qs, gs, segq, ls, ds, dq, dkv, kv = refs
    load_pieces(pieces, kv)
    dim = gain.shape[1]
    group = qproj.shape[1] // dim
    pairs = info.shape[0] - 1
    plain = dim ** (-0.5)
    factor = LOG2E * plain
    for head in range(group):
        cols = slice(head * dim, (head + 1) * dim)
        query = head_forward(qproj[:, cols], gain[...], cosine[...], sine[...])[0]
        delta = jnp.sum(grad[:, cols].astype(F32) * wide[:, cols], axis=-1, keepdims=True)
        for piece in range(2):
            spot = slice(head * half, (head + 1) * half)
            rows = slice(piece * half, (piece + 1) * half)
            qs[piece, spot, :] = query[rows]
            gs[piece, spot, :] = grad[rows, cols]
            segq[piece, spot, :] = seg_col[rows, :1]
            ls[piece, spot, :] = logs[rows, head * dim : head * dim + 1]
            ds[piece, spot, :] = delta[rows]
    dq[...] = jnp.zeros_like(dq)
    dkv[...] = jnp.zeros_like(dkv)
    for step in range(pairs):
        piece, key_block, query_block, spot = pair_of(info, step)
        rows = pl.ds(pl.multiple_of(spot * half, half), half)
        query, outer = qs[piece], gs[piece]
        scores = dot_right_t(query, kv[rows, :dim])
        key_seg = seg_row[:, pl.ds(pl.multiple_of(key_block * half, half), half)]
        allowed = allowed_pair(scores.shape, half, query_block, key_block, segq[piece], key_seg)
        prob = jnp.where(allowed, jnp.exp2(scores * factor - ls[piece]), 0.0)
        dprob = dot_right_t(outer, kv[rows, dim:])
        dscores = (prob * (dprob - ds[piece])).astype(LOW)
        dq[piece] += dot_plain(dscores, kv[rows, :dim])
        dkv[rows, :dim] += dot_left_t(dscores, query)
        dkv[rows, dim:] += dot_left_t(prob.astype(LOW), outer)
    rows = 2 * half
    for at in range(count):
        target = send_out if at % 2 else keep_out
        spot, low = slice(at // 2 * rows, (at // 2 + 1) * rows), slice(at * rows, (at + 1) * rows)
        target[spot, :dim] = (dkv[low, :dim] * plain).astype(LOW)
        target[spot, dim:] = dkv[low, dim:].astype(LOW)
    total = jnp.zeros(norm_out.shape[1:], F32)
    for head in range(group):
        cols = slice(head * dim, (head + 1) * dim)
        scale = rms_scale(qproj[:, cols])
        unit = qproj[:, cols] * scale
        grads = jnp.concatenate([dq[piece, head * half : (head + 1) * half, :] for piece in range(2)]) * plain
        back, norm = head_backward(grads, unit, scale, gain[...], cosine[...], sine[...])
        total = total + norm
        dq_out[:, cols] = back
    norm_out[0] = total


def heads_spec(rows, width):
    return pl.BlockSpec((rows, width), lambda head, *_: (0, head))


def attend(info, qproj, weights, pieces, gain, cosine, sine, seg_row, seg_col):
    rows, qcols = qproj.shape
    count, kvcols = len(pieces), pieces[0].shape[1]
    dim = gain.shape[1]
    heads = kvcols // (2 * dim)
    stacked = rows // 2 * (qcols // (heads * dim))
    early = [pltpu.with_memory_space_constraint(item, pltpu.VMEM) for item in (qproj, cosine, sine, seg_col)]
    qproj, cosine, sine, seg_col = early
    operands = [qproj, *weights, *pieces, gain, cosine, sine, seg_row, seg_col]
    in_vmem = pl.BlockSpec(memory_space=pltpu.VMEM)
    width = sum(item.shape[0] for item in weights)
    shapes = [((rows, qcols), LOW), ((rows, qcols), F32), ((rows, qcols), F32), ((rows, width), LOW)]
    return pl.pallas_call(
        functools.partial(attend_kernel, rows // 2, count, len(weights)),
        grid_spec=pltpu.PrefetchScalarGridSpec(
            num_scalar_prefetch=1,
            grid=(1,),
            in_specs=[in_vmem if any(item is one for one in early) else whole(item.shape) for item in operands],
            out_specs=[whole(shape) for shape, _ in shapes],
            scratch_shapes=[
                pltpu.VMEM((heads, 2, stacked, dim), LOW),
                pltpu.VMEM((heads, 2, stacked, dim), F32),
                pltpu.VMEM((heads, 2, stacked, 128), F32),
                pltpu.VMEM((2, stacked, 1), jnp.int32),
                pltpu.VMEM((count * rows, kvcols), LOW),
            ],
        ),
        out_shape=[jax.ShapeDtypeStruct(shape, kind) for shape, kind in shapes],
        compiler_params=params(44),
        cost_estimate=cost(2 * rows * count * rows * qcols * 2, 8 * rows * qcols * 2),
    )(info, *operands)


def attend_back(info, qproj, wide_out, logs, grad, pieces, gain, cosine, sine, seg_row, seg_col):
    rows, qcols = qproj.shape
    count, kvcols = len(pieces), pieces[0].shape[1]
    dim = gain.shape[1]
    heads = kvcols // (2 * dim)
    wide = qcols // heads
    half = rows // 2
    stacked = half * (wide // dim)
    qspec, kspec = heads_spec(rows, wide), heads_spec(rows, 2 * dim)
    part = heads_spec(count // 2 * rows, 2 * dim)
    tables = (gain, cosine, sine, seg_row, seg_col)
    return pl.pallas_call(
        functools.partial(attend_back_kernel, half, count),
        grid_spec=pltpu.PrefetchScalarGridSpec(
            num_scalar_prefetch=1,
            grid=(heads,),
            in_specs=[qspec] * 4 + [kspec] * count + [whole(item.shape) for item in tables],
            out_specs=[qspec, part, part, pl.BlockSpec((1, 8, dim), lambda head, *_: (head, 0, 0))],
            scratch_shapes=[
                pltpu.VMEM((2, stacked, dim), LOW),
                pltpu.VMEM((2, stacked, dim), LOW),
                pltpu.VMEM((2, stacked, 1), jnp.int32),
                pltpu.VMEM((2, stacked, 1), F32),
                pltpu.VMEM((2, stacked, 1), F32),
                pltpu.VMEM((2, stacked, dim), F32),
                pltpu.VMEM((count * rows, 2 * dim), F32),
                pltpu.VMEM((count * rows, 2 * dim), LOW),
            ],
        ),
        out_shape=[
            jax.ShapeDtypeStruct((rows, qcols), LOW),
            jax.ShapeDtypeStruct((count // 2 * rows, kvcols), LOW),
            jax.ShapeDtypeStruct((count // 2 * rows, kvcols), LOW),
            jax.ShapeDtypeStruct((heads, 8, dim), F32),
        ],
        compiler_params=params(),
        cost_estimate=cost(0, rows * qcols),
    )(info, qproj, wide_out, logs, grad, *pieces, *tables)


def assemble_kernel(dim, key, value, query, out):
    kcols = key.shape[1]
    for head in range(kcols // dim):
        spot = slice(head * dim, (head + 1) * dim)
        out[:, 2 * head * dim : (2 * head + 1) * dim] = key[:, spot]
        out[:, (2 * head + 1) * dim : (2 * head + 2) * dim] = value[:, spot]
    out[:, 2 * kcols :] = query[...]


def assemble(key, value, query, dim):
    cols = 2 * key.shape[1] + query.shape[1]
    return pl.pallas_call(
        functools.partial(assemble_kernel, dim),
        out_shape=jax.ShapeDtypeStruct((key.shape[0], cols), LOW),
        compiler_params=params(),
        cost_estimate=cost(0, 4 * key.shape[0] * cols),
    )(key, value, query)


def opening(inputs, halves, kvcols, qcols, kgain, cosine, sine):
    rows, width = inputs.shape
    tile = min(256, rows)
    shapes = [(kvcols, F32), (qcols, F32), (kvcols, LOW)]

    def tiled(cols):
        return pl.BlockSpec((tile, cols), lambda step: (step, 0))

    return pl.pallas_call(
        functools.partial(opening_kernel, len(halves)),
        grid=(rows // tile,),
        in_specs=[tiled(width)]
        + [whole(item.shape) for item in halves]
        + [whole(kgain.shape), tiled(cosine.shape[1]), tiled(sine.shape[1])],
        out_specs=[tiled(cols) for cols, _ in shapes],
        out_shape=[jax.ShapeDtypeStruct((rows, cols), kind) for cols, kind in shapes],
        compiler_params=params(28),
        cost_estimate=cost(2 * rows * width * (kvcols + qcols), 4 * rows * width + 2 * width * kvcols),
    )(inputs, *halves, kgain, cosine, sine)


def key_backward(mine, other, proj, gain, cosine, sine):
    return pl.pallas_call(
        key_backward_kernel,
        out_shape=[
            jax.ShapeDtypeStruct(proj.shape, LOW),
            jax.ShapeDtypeStruct((8, gain.shape[1]), F32),
        ],
        compiler_params=params(),
        cost_estimate=cost(0, proj.size),
    )(mine, other, proj, gain, cosine, sine)


def feed_kernel(
    ids, hidden, attn, gain, weights, dproduct, product, dgate, dup, dinputs, middle_out, inputs_out,
    total, both, middle, inputs, sems,
):
    tile = dproduct.shape[1]
    step = pl.program_id(0)
    copies = [
        pltpu.make_async_copy(middle, middle_out, sems.at[0]),
        pltpu.make_async_copy(inputs, inputs_out, sems.at[1]),
    ]

    @pl.when(step == 0)
    def _():
        second_norm_kernel(gain.shape[0], ids, hidden, attn, gain, middle, inputs)
        for copy in copies:
            copy.start()
        total[...] = jnp.zeros_like(total)

    ins = dot_plain(inputs[...], weights[...])
    gate_in, up_in = ins[:, :tile], ins[:, tile:]
    sigmoid = 1.0 / (1.0 + jnp.exp(-gate_in))
    active = gate_in * sigmoid
    product[...] = (active * up_in).astype(LOW)
    grad = dproduct[...]
    dgate_low = (grad * up_in * sigmoid * (1.0 + gate_in * (1.0 - sigmoid))).astype(LOW)
    dup_low = (grad * active).astype(LOW)
    dgate[...] = dgate_low
    dup[...] = dup_low
    both[:, :tile] = dgate_low
    both[:, tile:] = dup_low
    total[...] += dot_right_t(both[...], weights[...])

    @pl.when(step == pl.num_programs(0) - 1)
    def _():
        dinputs[...] = total[...].astype(LOW)
        for copy in copies:
            copy.wait()


def feed_tile(units):
    return 256 if units % 256 == 0 else units


def by_tiles(gate, up):
    rows, units = gate.shape
    tile = feed_tile(units)

    def kernel(gate_ref, up_ref, out):
        for at in range(0, units, tile):
            out[:, 2 * at : 2 * at + tile] = gate_ref[:, at : at + tile]
            out[:, 2 * at + tile : 2 * at + 2 * tile] = up_ref[:, at : at + tile]

    return pl.pallas_call(
        kernel,
        out_shape=jax.ShapeDtypeStruct((rows, 2 * units), gate.dtype),
        compiler_params=params(),
        cost_estimate=cost(0, 8 * rows * units),
    )(gate, up)


def feed(ids, hidden, attn, gain, gate_up, dproduct):
    rows, width = hidden.shape
    units = dproduct.shape[1]
    tile = feed_tile(units)
    tspec = pl.BlockSpec((rows, tile), lambda step, *_: (0, step))
    anywhere = pl.BlockSpec(memory_space=pl.ANY)
    return pl.pallas_call(
        feed_kernel,
        grid_spec=pltpu.PrefetchScalarGridSpec(
            num_scalar_prefetch=1,
            grid=(units // tile,),
            in_specs=[whole((rows, width)), whole((rows, width)), whole(gain.shape)]
            + [pl.BlockSpec((width, 2 * tile), lambda step, *_: (0, step)), tspec],
            out_specs=[tspec, tspec, tspec, whole((rows, width)), anywhere, anywhere],
            scratch_shapes=[
                pltpu.VMEM((rows, width), F32),
                pltpu.VMEM((rows, 2 * tile), LOW),
                pltpu.VMEM((rows, width), F32),
                pltpu.VMEM((rows, width), LOW),
                pltpu.SemaphoreType.DMA((2,)),
            ],
        ),
        out_shape=[jax.ShapeDtypeStruct((rows, units), LOW)] * 3
        + [jax.ShapeDtypeStruct((rows, width), kind) for kind in (LOW, F32, LOW)],
        compiler_params=params(),
        cost_estimate=cost(8 * rows * width * units, 4 * width * units + 10 * rows * units),
    )(ids, hidden, attn, gain, gate_up, dproduct)


def shards(
    hidden_in,
    segments,
    cotangent,
    attn_gain,
    query_weight,
    key_weight,
    value_weight,
    output_weight,
    qnorm_gain,
    knorm_gain,
    ffn_gain,
    gate_weight,
    up_weight,
    down_weight,
):
    is_staged = lax.axis_size("fsdp") == 2 and lax.axis_size("context") == 4
    gather_fast = staged_gather if is_staged else gather_rows
    scatter_fast = staged_scatter if is_staged else scatter_rows
    head_dim = qnorm_gain.shape[0]
    local_rows, width = hidden_in.shape
    shard_rows = query_weight.shape[0]
    pieces = lax.axis_size("context")
    total_rows = local_rows * pieces
    half_rows = local_rows // 2
    value_heads = key_weight.shape[1] // head_dim
    qcols = query_weight.shape[1]
    kcols = key_weight.shape[1]

    def unmixed(both, which):
        starts = [(2 * head + which) * head_dim for head in range(value_heads)]
        return jnp.concatenate([both[:, at : at + head_dim] for at in starts], axis=1)

    blocks = staged_blocks() if is_staged else jnp.zeros((1,), jnp.int32)
    count = blocks.shape[0]
    near_shard = assemble(key_weight, value_weight, query_weight, head_dim)
    gain_shard, near_shard = tie(jnp.stack([attn_gain, ffn_gain]), near_shard)
    gains = gather_fast(gain_shard).reshape(-1, 2, shard_rows).astype(F32)
    gain_one = gains[:, 0].reshape(count, -1)
    gain_two = gains[:, 1].reshape(count, -1)

    me = lax.axis_index("context")
    last = 2 * pieces - 1
    spots = []
    for block in range(2 * pieces):
        owner = block if block < pieces else last - block
        spots.append(2 * (owner ^ me) + (0 if block < pieces else 1))
    info = jnp.stack([me, last - me] + spots).astype(jnp.int32)
    ramp = jnp.arange(half_rows, dtype=jnp.int32)
    positions = jnp.concatenate([me * half_rows + ramp, (last - me) * half_rows + ramp])
    seg_col = jnp.concatenate(
        [
            lax.dynamic_slice_in_dim(segments[0], block * half_rows, half_rows)
            for block in (me, last - me)
        ]
    )[:, None]
    seg_col = jnp.broadcast_to(seg_col, (local_rows, head_dim))
    half_dim = head_dim // 2
    inverse = THETA ** (-(jnp.arange(half_dim).astype(F32) * 2.0 / head_dim))
    angles = positions.astype(F32)[:, None] * inverse[None, :]
    cosine = jnp.cos(angles)
    sine = jnp.sin(angles)
    cosine = jnp.concatenate([cosine, cosine], axis=1)
    sine = jnp.concatenate([-sine, sine], axis=1)
    qgain = qnorm_gain.astype(F32)[None, :]
    kgain = knorm_gain.astype(F32)[None, :]

    (cot_staged,) = row_call(stage_kernel, blocks, [cotangent], [LOW])
    out_blocks = staged_blocks("y") if is_staged else blocks
    if is_staged:
        match = (out_blocks[:, None] == blocks[None, :]).astype(F32)
        gain_two = jnp.dot(match, gain_two, precision=lax.Precision.HIGHEST)
    if is_staged:
        near_pair = staged_pair(near_shard)
        near_far = staged(near_pair, "yx")
        near_far, gain_one = tie(near_far, gain_one)
        near_last, out_shard = tie(staged(near_far, "core"), output_weight)
        near_halves = [near_pair, near_far, staged(near_pair, "core"), near_last]
        out_pair = staged_pair(out_shard, "y")
    else:
        near_halves = [gather_rows(near_shard)]
    (inputs_one,) = row_call(first_norm_kernel, blocks, [hidden_in], [LOW], gain_one, [info, seg_col, cosine, sine, qgain, kgain, gain_two], mib=20)
    kv_proj, query_proj, kv_own = opening(inputs_one, near_halves, 2 * kcols, qcols, kgain, cosine, sine)
    if is_staged:
        out_pair, kv_own = tie(out_pair, kv_own)
        out_halves = staged_halves(staged_quad(out_pair, "y"))
    else:
        out_halves = [gather_rows(output_weight)]
    kv_across = swap_context(kv_own, 2)
    kv_pieces = [kv_own, swap_context(kv_own, 1), kv_across, swap_context(kv_across, 1)]
    gate_up_shard, kv_proj = tie(by_tiles(gate_weight, up_weight), kv_proj)
    gate_up = gather_rows(gate_up_shard)
    attended, attended_wide, logs, attn_part = attend(
        info, query_proj, out_halves, kv_pieces, qgain, cosine, sine, segments, seg_col
    )
    down_shard, logs = tie(down_weight, logs)
    down_full = gather_fast(down_shard)
    attn_out = sum_tensor(attn_part)
    dproduct = dot_plain(cot_staged, down_full)
    near_full = jnp.concatenate(near_halves)
    out_full = jnp.concatenate(out_halves)
    attn_out, dproduct, near_full, out_full = tie(attn_out, dproduct, near_full, out_full)
    product, dgate, dup_low, dnormed_two_part, middle, inputs_two = feed(
        out_blocks, hidden_in, attn_out, gain_two, gate_up, dproduct
    )
    dnormed_two = sum_tensor(dnormed_two_part)

    ffn_part = dot_right_t(product, down_full).astype(LOW)
    down_own = scatter_rows(dot_left_t(cotangent, product))
    grad_gate = dot_left_t(inputs_two, dgate).astype(LOW)
    grad_up = dot_left_t(inputs_two, dup_low).astype(LOW)
    dnormed_two, ffn_part, grad_gate, grad_up = tie(dnormed_two, ffn_part, grad_gate, grad_up)
    ffn_out = sum_tensor(ffn_part)
    dmiddle, dattn, gain_two_sums = row_call(
        second_back_kernel, out_blocks, [dnormed_two, middle, cotangent], [F32, LOW], gain_two, sums=True
    )
    gain_two_part = jnp.sum(gain_two_sums, axis=0) / lax.axis_size("tensor")
    dattended = dot_plain(dattn, out_full).astype(LOW)
    dquery, dkv_keep, dkv_send, qnorm_parts = attend_back(
        info, query_proj, attended_wide, logs, dattended, kv_pieces, qgain, cosine, sine, segments, seg_col
    )
    grad_gate, down_own, qnorm_parts = tie(grad_gate, down_own, qnorm_parts)
    gate_own = scatter_rows(grad_gate)
    dkv_pair = add_low(dkv_keep, swap_context(dkv_send, 1))
    dkv, knorm_parts = key_backward(
        dkv_pair[:local_rows], swap_context(dkv_pair[local_rows:], 2), kv_proj, kgain, cosine, sine
    )
    grad_output = dot_left_t(dattn, attended).astype(LOW)
    output_own = staged_scatter(grad_output, "y") if is_staged else scatter_rows(grad_output)
    dqkv = jnp.concatenate([dkv, dquery], axis=1)
    dnormed_one_part = dot_right_t(dqkv, near_full).astype(LOW)
    later_part, ffn_out = tie(dnormed_one_part, ffn_out)
    dnormed_one = sum_tensor(later_part)
    grad_up, gate_own, ffn_out = tie(grad_up, gate_own, ffn_out)
    (output,) = row_call(output_kernel, blocks, [middle, ffn_out], [LOW])
    qkv_own = scatter_fast(dot_left_t(inputs_one, dqkv).astype(LOW))
    gain_one_part = jnp.sum(dnormed_one_part.astype(F32) * inputs_one.astype(F32), axis=0)
    up_own = scatter_rows(grad_up)
    if is_staged:
        onehot = (blocks[None, :] == jnp.arange(count, dtype=jnp.int32)[:, None]).astype(F32)
        gain_one_part = jnp.dot(
            onehot, gain_one_part.reshape(count, -1), precision=lax.Precision.HIGHEST
        ).reshape(-1)
    small = sum_all(
        jnp.concatenate(
            [gain_one_part, gain_two_part, jnp.sum(qnorm_parts, axis=(0, 1)), jnp.sum(knorm_parts, axis=0)]
        )
    )
    own = attn_gain.shape[0]
    start = lax.axis_index(ROWS) * own
    gain_one_grad = lax.dynamic_slice_in_dim(small[:width], start, own) / attn_gain.astype(F32)
    gain_two_grad = lax.dynamic_slice_in_dim(small[width : 2 * width], start, own)
    qnorm_total = small[2 * width : 2 * width + head_dim]
    knorm_total = small[2 * width + head_dim :]
    qkv_own = qkv_own.astype(F32)
    query_grad = qkv_own[:, 2 * kcols :]
    key_grad, value_grad = unmixed(qkv_own, 0), unmixed(qkv_own, 1)
    output_own = output_own.astype(F32)
    gate_own = gate_own.astype(F32)
    down_own = down_own.astype(F32)
    done = [output, small, query_grad, key_grad, value_grad, output_own, gate_own, down_own]
    (input_grad,) = row_call(
        first_back_kernel, blocks, [dnormed_one, hidden_in, dmiddle], [F32], gain_one, after=done
    )
    return (
        output,
        input_grad,
        gain_one_grad,
        query_grad,
        key_grad,
        value_grad,
        output_own,
        qnorm_total,
        knorm_total,
        gain_two_grad,
        gate_own,
        up_own.astype(F32),
        down_own,
    )


def solution(mesh):
    in_specs = (
        P(("fsdp", "context"), None),
        P("fsdp", None),
        P(("fsdp", "context"), None),
        P(("fsdp", "context")),
        P(("fsdp", "context"), "tensor"),
        P(("fsdp", "context"), "tensor"),
        P(("fsdp", "context"), "tensor"),
        P(("fsdp", "context"), "tensor"),
        P(),
        P(),
        P(("fsdp", "context")),
        P(("fsdp", "context"), "tensor"),
        P(("fsdp", "context"), "tensor"),
        P(("fsdp", "context"), "tensor"),
    )
    out_specs = (
        P(("fsdp", "context"), None),
        P(("fsdp", "context"), None),
        P(("fsdp", "context")),
        P(("fsdp", "context"), "tensor"),
        P(("fsdp", "context"), "tensor"),
        P(("fsdp", "context"), "tensor"),
        P(("fsdp", "context"), "tensor"),
        P(),
        P(),
        P(("fsdp", "context")),
        P(("fsdp", "context"), "tensor"),
        P(("fsdp", "context"), "tensor"),
        P(("fsdp", "context"), "tensor"),
    )
    return jax.shard_map(shards, mesh=mesh, in_specs=in_specs, out_specs=out_specs, check_vma=False)
```

```python
import functools

import jax
import jax.numpy as jnp
from jax import lax
from jax.experimental import pallas as pl
from jax.experimental.pallas import tpu as pltpu
from jax.sharding import PartitionSpec as P

EPS = 1e-06
THETA = 1000000.0
ROWS = ("fsdp", "context")
LOW = jnp.bfloat16
F32 = jnp.float32
LOG2E = 1.4426950408889634
VMEM_MIB = 56


def dot_plain(matrix_a, matrix_b):
    return jnp.dot(matrix_a, matrix_b, preferred_element_type=F32)


def dot_right_t(matrix_a, matrix_b):
    return lax.dot_general(matrix_a, matrix_b, (((1,), (1,)), ((), ())), preferred_element_type=F32)


def dot_left_t(matrix_a, matrix_b):
    return lax.dot_general(matrix_a, matrix_b, (((0,), (0,)), ((), ())), preferred_element_type=F32)


def tie(*items):
    return lax.optimization_barrier(items)


def rms_scale(values):
    return lax.rsqrt(jnp.mean(values * values, axis=-1, keepdims=True) + EPS)


def gather_rows(shard):
    return lax.all_gather(shard, ROWS, axis=0, tiled=True)


def scatter_rows(full):
    return lax.psum_scatter(full.astype(LOW), ROWS, scatter_dimension=0, tiled=True)


def sum_tensor(partial):
    return lax.psum(partial.astype(LOW), "tensor")


def add_low(mine, other):
    return (mine.astype(F32) + other.astype(F32)).astype(LOW)


def place(index):
    return index // 4, (index // 2) % 2, index % 2


def staged_pairs(step):
    pairs = []
    for index in range(8):
        x, y, core = place(index)
        if step == "core":
            core = 1 - core
        elif step[core % len(step)] == "x":
            x = 1 - x
        else:
            y = 1 - y
        pairs.append((index, x * 4 + y * 2 + core))
    return pairs


def staged(values, step):
    return lax.ppermute(values, ROWS, staged_pairs(step))


def staged_block(index, step, first="xy"):
    x, y, core = place(index)
    d_core, d_second, d_first = step // 4, (step // 2) % 2, step % 2
    its_core = core ^ d_core
    x_first = 1 - its_core if first == "xy" else int(first == "x")
    its_x = x ^ (x_first * d_first + (1 - x_first) * d_second)
    its_y = y ^ (x_first * d_second + (1 - x_first) * d_first)
    return its_x * 4 + its_y * 2 + its_core


def staged_blocks(first="xy"):
    index = lax.axis_index(ROWS)
    return jnp.stack([staged_block(index, step, first) for step in range(8)]).astype(jnp.int32)


def staged_direct(shard):
    parts = [shard]
    for step in range(1, 8):
        parts.append(lax.ppermute(shard, ROWS, [(staged_block(index, step), index) for index in range(8)]))
    return jnp.concatenate(parts)


OTHER = {"xy": "yx", "yx": "xy", "x": "y", "y": "x"}


def staged_pair(shard, first="xy"):
    return jnp.concatenate([shard, staged(shard, first)])


def staged_quad(pair, first="xy"):
    return jnp.concatenate([pair, staged(pair, OTHER[first])])


def staged_halves(quad):
    return [quad, staged(quad, "core")]


def staged_gather(shard):
    return jnp.concatenate(staged_halves(staged_quad(staged_pair(shard))))


def staged_scatter(full, first="xy"):
    rows = full.shape[0] // 8
    quad = add_low(full[: 4 * rows], staged(full[4 * rows :], "core"))
    pair = add_low(quad[: 2 * rows], staged(quad[2 * rows :], OTHER[first]))
    return pair[:rows].astype(F32) + staged(pair[rows:], first).astype(F32)


def sum_all(values):
    for axis in ("tensor", "context", "fsdp"):
        size = lax.axis_size(axis)
        if size & (size - 1):
            values = lax.psum(values, axis)
            continue
        bit = 1
        while bit < size:
            values = values + lax.ppermute(values, axis, [(index, index ^ bit) for index in range(size)])
            bit *= 2
    return values


def swap_context(values, bit):
    size = lax.axis_size("context")
    return lax.ppermute(values, "context", [(index, index ^ bit) for index in range(size)])


def params(mib=VMEM_MIB):
    return pltpu.CompilerParams(vmem_limit_bytes=mib * 1024 * 1024)


def cost(flops, moved):
    return pl.CostEstimate(flops=int(flops), bytes_accessed=int(moved), transcendentals=0)


def whole(shape):
    return pl.BlockSpec(shape, lambda *_: (0,) * len(shape))


def column(ids, step, width):
    return pl.ds(pl.multiple_of(ids[step] * width, width), width)


def stage_kernel(count, ids, values, staged_out):
    width = values.shape[1] // count
    for step in range(count):
        staged_out[:, step * width : (step + 1) * width] = values[:, column(ids, step, width)]


def by_rows(rows, body):
    def run(step, carry):
        body(pl.ds(pl.multiple_of(step * 16, 16), 16))
        return carry

    lax.fori_loop(0, rows // 16, run, 0, unroll=4)


def row_sum(parts):
    return jnp.sum(sum(parts), axis=-1, keepdims=True)


def scale_of(parts):
    size = len(parts) * parts[0].shape[1]
    return lax.rsqrt(row_sum([part * part for part in parts]) / size + EPS)


def first_norm_kernel(count, ids, hidden, gain, staged_out):
    width = hidden.shape[1] // count
    spots = [column(ids, step, width) for step in range(count)]

    def body(rows):
        parts = [hidden[rows, spot].astype(F32) for spot in spots]
        scale = scale_of(parts)
        for step in range(count):
            part = parts[step] * scale * gain[step : step + 1, :]
            staged_out[rows, step * width : (step + 1) * width] = part.astype(LOW)

    by_rows(hidden.shape[0], body)


def second_norm_kernel(count, ids, hidden, attn, gain, middle, plain_out):
    width = hidden.shape[1] // count
    spots = [column(ids, step, width) for step in range(count)]

    def body(rows):
        parts = []
        for step in range(count):
            part = attn[rows, step * width : (step + 1) * width].astype(F32)
            parts.append(hidden[rows, spots[step]].astype(F32) + part)
            middle[rows, spots[step]] = parts[step]
        scale = scale_of(parts)
        for step in range(count):
            plain_out[rows, spots[step]] = (parts[step] * scale * gain[step : step + 1, :]).astype(LOW)

    by_rows(hidden.shape[0], body)


def output_kernel(count, ids, middle, ffn, out):
    width = middle.shape[1] // count
    for step in range(count):
        spot = column(ids, step, width)
        out[:, spot] = (middle[:, spot] + ffn[:, step * width : (step + 1) * width].astype(F32)).astype(LOW)


def second_back_kernel(count, ids, grad, middle, cotangent, gain, dmiddle, staged_out, gain_out):
    width = middle.shape[1] // count

    @pl.when(pl.program_id(0) == 0)
    def _():
        gain_out[...] = jnp.zeros_like(gain_out)

    spots = [column(ids, step, width) for step in range(count)]

    def body(rows):
        parts = [middle[rows, spot] for spot in spots]
        raw = [grad[rows, spot].astype(F32) for spot in spots]
        grads = [raw[step] * gain[step : step + 1, :] for step in range(count)]
        scale = scale_of(parts)
        mean = row_sum([one * two for one, two in zip(parts, grads)]) * scale * scale / middle.shape[1]
        for step in range(count):
            term = raw[step] * parts[step] * scale
            gain_out[:, spots[step]] += term[:8] + term[8:]
            part = cotangent[rows, spots[step]].astype(F32) + scale * (grads[step] - parts[step] * mean)
            dmiddle[rows, spots[step]] = part.astype(LOW)
            staged_out[rows, step * width : (step + 1) * width] = part.astype(LOW)

    by_rows(middle.shape[0], body)


def first_back_kernel(count, ids, grad, hidden, dmiddle, gain, out):
    width = hidden.shape[1] // count
    spots = [column(ids, step, width) for step in range(count)]

    def body(rows):
        parts = [hidden[rows, spot].astype(F32) for spot in spots]
        grads = [
            grad[rows, step * width : (step + 1) * width].astype(F32) * gain[step : step + 1, :]
            for step in range(count)
        ]
        scale = scale_of(parts)
        mean = row_sum([one * two for one, two in zip(parts, grads)]) * scale * scale / hidden.shape[1]
        for step in range(count):
            term = dmiddle[rows, spots[step]].astype(F32)
            out[rows, spots[step]] = term + scale * (grads[step] - parts[step] * mean)

    by_rows(hidden.shape[0], body)


def row_call(kernel, ids, arrays, out_types, gain=None, after=(), sums=False, mib=VMEM_MIB):
    rows, width = arrays[0].shape
    tile = min(256, rows)
    spec = pl.BlockSpec((tile, width), lambda step, *_: (step, 0))
    moved = sum(item.size * item.dtype.itemsize for item in arrays) + sum(
        rows * width * jnp.dtype(kind).itemsize for kind in out_types
    )
    gains = [] if gain is None else [gain]

    def ordered(ids, *refs):
        kernel(ids.shape[0], ids, *refs[len(after) :])

    return pl.pallas_call(
        ordered,
        grid_spec=pltpu.PrefetchScalarGridSpec(
            num_scalar_prefetch=1,
            grid=(rows // tile,),
            in_specs=[pl.BlockSpec(memory_space=pl.ANY)] * len(after)
            + [spec] * len(arrays)
            + [whole(item.shape) for item in gains],
            out_specs=[spec] * len(out_types) + [whole((8, width))] * sums,
        ),
        out_shape=[jax.ShapeDtypeStruct((rows, width), kind) for kind in out_types]
        + [jax.ShapeDtypeStruct((8, width), F32)] * sums,
        compiler_params=params(mib),
        cost_estimate=cost(10 * rows * width, moved),
    )(ids, *after, *arrays, *gains)


def rotate(values, cosine, sine):
    return values * cosine + pltpu.roll(values, values.shape[1] // 2, 1) * sine


def head_forward(proj, gain, cosine, sine):
    scale = rms_scale(proj)
    unit = proj * scale
    return rotate(unit * gain, cosine, sine).astype(LOW), unit, scale


def head_backward(grad, unit, scale, gain, cosine, sine):
    turned = rotate(grad.astype(LOW).astype(F32), cosine, -sine)
    scaled = turned * gain
    back = scale * (scaled - unit * jnp.mean(scaled * unit, axis=-1, keepdims=True))
    rows, width = grad.shape
    return back.astype(LOW), jnp.sum((turned * unit).reshape(rows // 8, 8, width), axis=0)


def opening_kernel(parts_in, inputs, *refs):
    weights, refs = refs[:parts_in], refs[parts_in:]
    kgain, cosine, sine, proj, qproj, out = refs
    dim = kgain.shape[1]
    kvcols, qcols = proj.shape[1], qproj.shape[1]

    def project(cols):
        total = jnp.zeros((inputs.shape[0], cols.stop - cols.start), F32)
        for step, source in enumerate(weights):
            deep = source.shape[0]
            total = total + dot_plain(inputs[:, step * deep : (step + 1) * deep], source[:, cols])
        return total

    total = project(slice(0, kvcols))
    proj[...] = total
    for head in range(kvcols // (2 * dim)):
        at = 2 * head * dim
        out[:, at : at + dim] = head_forward(total[:, at : at + dim], kgain[...], cosine[...], sine[...])[0]
        out[:, at + dim : at + 2 * dim] = total[:, at + dim : at + 2 * dim].astype(LOW)
    qproj[...] = project(slice(kvcols, kvcols + qcols))


def key_backward_kernel(mine, other, proj, gain, cosine, sine, out, norm_out):
    dim = gain.shape[1]
    total = jnp.zeros(norm_out.shape, F32)
    for head in range(proj.shape[1] // (2 * dim)):
        at = 2 * head * dim
        scale = rms_scale(proj[:, at : at + dim])
        unit = proj[:, at : at + dim] * scale
        grad = mine[:, at : at + dim].astype(F32) + other[:, at : at + dim].astype(F32)
        back, norm = head_backward(grad, unit, scale, gain[...], cosine[...], sine[...])
        total = total + norm
        out[:, at : at + dim] = back
        spot = slice(at + dim, at + 2 * dim)
        out[:, spot] = (mine[:, spot].astype(F32) + other[:, spot].astype(F32)).astype(LOW)
    norm_out[...] = total


def pair_of(info, step):
    first = info[0]
    late = step > first
    piece = jnp.where(late, 1, 0)
    key_block = jnp.where(late, step - first - 1, step)
    query_block = jnp.where(late, info[1], first)
    return piece, key_block, query_block, info[2 + key_block]


def allowed_pair(shape, half, query_block, key_block, query_seg, key_seg):
    row = lax.rem(lax.broadcasted_iota(jnp.int32, shape, 0), half)
    col = lax.broadcasted_iota(jnp.int32, shape, 1)
    return (col - row <= (query_block - key_block) * half) & (query_seg == key_seg)


def load_pieces(pieces, kv):
    rows = pieces[0].shape[0]
    for place_at, piece in enumerate(pieces):
        kv[place_at * rows : (place_at + 1) * rows, :] = piece[...]


def attend_kernel(half, count, parts_in, info, qproj, *refs):
    weights, refs = refs[:parts_in], refs[parts_in:]
    pieces, (gain, cosine, sine, seg_row, seg_col), refs = refs[:count], refs[count : count + 5], refs[count + 5 :]
    out, out_wide, log_out, part_out, qs, acc, total, segq, kv = refs
    load_pieces(pieces, kv)
    dim = gain.shape[1]
    heads = kv.shape[1] // (2 * dim)
    group = qproj.shape[1] // (dim * heads)
    pairs = info.shape[0] - 1
    factor = LOG2E * dim ** (-0.5)
    for piece in range(2):
        for member in range(group):
            segq[piece, member * half : (member + 1) * half, :] = seg_col[piece * half : (piece + 1) * half, :1]
    for head in range(heads):
        for member in range(group):
            at = (head * group + member) * dim
            query = head_forward(qproj[:, at : at + dim], gain[...], cosine[...], sine[...])[0]
            for piece in range(2):
                qs[head, piece, member * half : (member + 1) * half, :] = query[piece * half : (piece + 1) * half]
    acc[...] = jnp.zeros_like(acc)
    total[...] = jnp.zeros_like(total)
    for step in range(pairs):
        piece, key_block, query_block, spot = pair_of(info, step)
        rows = pl.ds(pl.multiple_of(spot * half, half), half)
        key_seg = seg_row[:, pl.ds(pl.multiple_of(key_block * half, half), half)]
        allowed = allowed_pair((group * half, half), half, query_block, key_block, segq[piece], key_seg)
        for head in range(heads):
            at = 2 * head * dim
            scores = dot_right_t(qs[head, piece], kv[rows, at : at + dim])
            weight = jnp.where(allowed, jnp.exp2(scores * factor), 0.0)
            total[head, piece] += sum(weight[:, col : col + 128] for col in range(0, half, 128))
            acc[head, piece] += dot_plain(weight.astype(LOW), kv[rows, at + dim : at + 2 * dim])
    for head in range(heads):
        for piece in range(2):
            sums = jnp.sum(total[head, piece], axis=-1, keepdims=True)
            result = acc[head, piece] / sums
            logs = jnp.broadcast_to(jnp.log2(sums), result.shape)
            rows = slice(piece * half, (piece + 1) * half)
            for member in range(group):
                at = (head * group + member) * dim
                part = result[member * half : (member + 1) * half]
                out[rows, at : at + dim] = part.astype(LOW)
                out_wide[rows, at : at + dim] = part
                log_out[rows, at : at + dim] = logs[member * half : (member + 1) * half]
    for step, source in enumerate(weights):
        cols = slice(step * source.shape[0], (step + 1) * source.shape[0])
        part_out[:, cols] = dot_right_t(out[...], source[...]).astype(LOW)


def attend_back_kernel(half, count, info, qproj, wide, logs, grad, *refs):
    pieces, (gain, cosine, sine, seg_row, seg_col), refs = refs[:count], refs[count : count + 5], refs[count + 5 :]
    dq_out, keep_out, send_out, norm_out, qs, gs, segq, ls, ds, dq, dkv, kv = refs
    load_pieces(pieces, kv)
    dim = gain.shape[1]
    group = qproj.shape[1] // dim
    pairs = info.shape[0] - 1
    plain = dim ** (-0.5)
    factor = LOG2E * plain
    for head in range(group):
        cols = slice(head * dim, (head + 1) * dim)
        query = head_forward(qproj[:, cols], gain[...], cosine[...], sine[...])[0]
        delta = jnp.sum(grad[:, cols].astype(F32) * wide[:, cols], axis=-1, keepdims=True)
        for piece in range(2):
            spot = slice(head * half, (head + 1) * half)
            rows = slice(piece * half, (piece + 1) * half)
            qs[piece, spot, :] = query[rows]
            gs[piece, spot, :] = grad[rows, cols]
            segq[piece, spot, :] = seg_col[rows, :1]
            ls[piece, spot, :] = logs[rows, head * dim : head * dim + 1]
            ds[piece, spot, :] = delta[rows]
    dq[...] = jnp.zeros_like(dq)
    dkv[...] = jnp.zeros_like(dkv)
    for step in range(pairs):
        piece, key_block, query_block, spot = pair_of(info, step)
        rows = pl.ds(pl.multiple_of(spot * half, half), half)
        query, outer = qs[piece], gs[piece]
        scores = dot_right_t(query, kv[rows, :dim])
        key_seg = seg_row[:, pl.ds(pl.multiple_of(key_block * half, half), half)]
        allowed = allowed_pair(scores.shape, half, query_block, key_block, segq[piece], key_seg)
        prob = jnp.where(allowed, jnp.exp2(scores * factor - ls[piece]), 0.0)
        dprob = dot_right_t(outer, kv[rows, dim:])
        dscores = (prob * (dprob - ds[piece])).astype(LOW)
        dq[piece] += dot_plain(dscores, kv[rows, :dim])
        dkv[rows, :dim] += dot_left_t(dscores, query)
        dkv[rows, dim:] += dot_left_t(prob.astype(LOW), outer)
    rows = 2 * half
    for at in range(count):
        target = send_out if at % 2 else keep_out
        spot, low = slice(at // 2 * rows, (at // 2 + 1) * rows), slice(at * rows, (at + 1) * rows)
        target[spot, :dim] = (dkv[low, :dim] * plain).astype(LOW)
        target[spot, dim:] = dkv[low, dim:].astype(LOW)
    total = jnp.zeros(norm_out.shape[1:], F32)
    for head in range(group):
        cols = slice(head * dim, (head + 1) * dim)
        scale = rms_scale(qproj[:, cols])
        unit = qproj[:, cols] * scale
        grads = jnp.concatenate([dq[piece, head * half : (head + 1) * half, :] for piece in range(2)]) * plain
        back, norm = head_backward(grads, unit, scale, gain[...], cosine[...], sine[...])
        total = total + norm
        dq_out[:, cols] = back
    norm_out[0] = total


def heads_spec(rows, width):
    return pl.BlockSpec((rows, width), lambda head, *_: (0, head))


def attend(info, qproj, weights, pieces, gain, cosine, sine, seg_row, seg_col):
    rows, qcols = qproj.shape
    count, kvcols = len(pieces), pieces[0].shape[1]
    dim = gain.shape[1]
    heads = kvcols // (2 * dim)
    stacked = rows // 2 * (qcols // (heads * dim))
    early = [pltpu.with_memory_space_constraint(item, pltpu.VMEM) for item in (qproj, cosine, sine, seg_col)]
    qproj, cosine, sine, seg_col = early
    operands = [qproj, *weights, *pieces, gain, cosine, sine, seg_row, seg_col]
    in_vmem = pl.BlockSpec(memory_space=pltpu.VMEM)
    width = sum(item.shape[0] for item in weights)
    shapes = [((rows, qcols), LOW), ((rows, qcols), F32), ((rows, qcols), F32), ((rows, width), LOW)]
    return pl.pallas_call(
        functools.partial(attend_kernel, rows // 2, count, len(weights)),
        grid_spec=pltpu.PrefetchScalarGridSpec(
            num_scalar_prefetch=1,
            grid=(1,),
            in_specs=[in_vmem if any(item is one for one in early) else whole(item.shape) for item in operands],
            out_specs=[whole(shape) for shape, _ in shapes],
            scratch_shapes=[
                pltpu.VMEM((heads, 2, stacked, dim), LOW),
                pltpu.VMEM((heads, 2, stacked, dim), F32),
                pltpu.VMEM((heads, 2, stacked, 128), F32),
                pltpu.VMEM((2, stacked, 1), jnp.int32),
                pltpu.VMEM((count * rows, kvcols), LOW),
            ],
        ),
        out_shape=[jax.ShapeDtypeStruct(shape, kind) for shape, kind in shapes],
        compiler_params=params(44),
        cost_estimate=cost(2 * rows * count * rows * qcols * 2, 8 * rows * qcols * 2),
    )(info, *operands)


def attend_back(info, qproj, wide_out, logs, grad, pieces, gain, cosine, sine, seg_row, seg_col):
    rows, qcols = qproj.shape
    count, kvcols = len(pieces), pieces[0].shape[1]
    dim = gain.shape[1]
    heads = kvcols // (2 * dim)
    wide = qcols // heads
    half = rows // 2
    stacked = half * (wide // dim)
    qspec, kspec = heads_spec(rows, wide), heads_spec(rows, 2 * dim)
    part = heads_spec(count // 2 * rows, 2 * dim)
    tables = (gain, cosine, sine, seg_row, seg_col)
    return pl.pallas_call(
        functools.partial(attend_back_kernel, half, count),
        grid_spec=pltpu.PrefetchScalarGridSpec(
            num_scalar_prefetch=1,
            grid=(heads,),
            in_specs=[qspec] * 4 + [kspec] * count + [whole(item.shape) for item in tables],
            out_specs=[qspec, part, part, pl.BlockSpec((1, 8, dim), lambda head, *_: (head, 0, 0))],
            scratch_shapes=[
                pltpu.VMEM((2, stacked, dim), LOW),
                pltpu.VMEM((2, stacked, dim), LOW),
                pltpu.VMEM((2, stacked, 1), jnp.int32),
                pltpu.VMEM((2, stacked, 1), F32),
                pltpu.VMEM((2, stacked, 1), F32),
                pltpu.VMEM((2, stacked, dim), F32),
                pltpu.VMEM((count * rows, 2 * dim), F32),
                pltpu.VMEM((count * rows, 2 * dim), LOW),
            ],
        ),
        out_shape=[
            jax.ShapeDtypeStruct((rows, qcols), LOW),
            jax.ShapeDtypeStruct((count // 2 * rows, kvcols), LOW),
            jax.ShapeDtypeStruct((count // 2 * rows, kvcols), LOW),
            jax.ShapeDtypeStruct((heads, 8, dim), F32),
        ],
        compiler_params=params(),
        cost_estimate=cost(0, rows * qcols),
    )(info, qproj, wide_out, logs, grad, *pieces, *tables)


def assemble_kernel(dim, key, value, query, out):
    kcols = key.shape[1]
    for head in range(kcols // dim):
        spot = slice(head * dim, (head + 1) * dim)
        out[:, 2 * head * dim : (2 * head + 1) * dim] = key[:, spot]
        out[:, (2 * head + 1) * dim : (2 * head + 2) * dim] = value[:, spot]
    out[:, 2 * kcols :] = query[...]


def assemble(key, value, query, dim):
    cols = 2 * key.shape[1] + query.shape[1]
    return pl.pallas_call(
        functools.partial(assemble_kernel, dim),
        out_shape=jax.ShapeDtypeStruct((key.shape[0], cols), LOW),
        compiler_params=params(),
        cost_estimate=cost(0, 4 * key.shape[0] * cols),
    )(key, value, query)


def opening(inputs, halves, kvcols, qcols, kgain, cosine, sine):
    rows, width = inputs.shape
    tile = min(256, rows)
    shapes = [(kvcols, F32), (qcols, F32), (kvcols, LOW)]

    def tiled(cols):
        return pl.BlockSpec((tile, cols), lambda step: (step, 0))

    return pl.pallas_call(
        functools.partial(opening_kernel, len(halves)),
        grid=(rows // tile,),
        in_specs=[tiled(width)]
        + [whole(item.shape) for item in halves]
        + [whole(kgain.shape), tiled(cosine.shape[1]), tiled(sine.shape[1])],
        out_specs=[tiled(cols) for cols, _ in shapes],
        out_shape=[jax.ShapeDtypeStruct((rows, cols), kind) for cols, kind in shapes],
        compiler_params=params(28),
        cost_estimate=cost(2 * rows * width * (kvcols + qcols), 4 * rows * width + 2 * width * kvcols),
    )(inputs, *halves, kgain, cosine, sine)


def key_backward(mine, other, proj, gain, cosine, sine):
    return pl.pallas_call(
        key_backward_kernel,
        out_shape=[
            jax.ShapeDtypeStruct(proj.shape, LOW),
            jax.ShapeDtypeStruct((8, gain.shape[1]), F32),
        ],
        compiler_params=params(),
        cost_estimate=cost(0, proj.size),
    )(mine, other, proj, gain, cosine, sine)


def feed_kernel(
    ids, hidden, attn, gain, weights, dproduct, product, dgate, dup, dinputs, middle_out, inputs_out,
    total, both, middle, inputs, sems,
):
    tile = dproduct.shape[1]
    step = pl.program_id(0)
    copies = [
        pltpu.make_async_copy(middle, middle_out, sems.at[0]),
        pltpu.make_async_copy(inputs, inputs_out, sems.at[1]),
    ]

    @pl.when(step == 0)
    def _():
        second_norm_kernel(gain.shape[0], ids, hidden, attn, gain, middle, inputs)
        for copy in copies:
            copy.start()
        total[...] = jnp.zeros_like(total)

    ins = dot_plain(inputs[...], weights[...])
    gate_in, up_in = ins[:, :tile], ins[:, tile:]
    sigmoid = 1.0 / (1.0 + jnp.exp(-gate_in))
    active = gate_in * sigmoid
    product[...] = (active * up_in).astype(LOW)
    grad = dproduct[...]
    dgate_low = (grad * up_in * sigmoid * (1.0 + gate_in * (1.0 - sigmoid))).astype(LOW)
    dup_low = (grad * active).astype(LOW)
    dgate[...] = dgate_low
    dup[...] = dup_low
    both[:, :tile] = dgate_low
    both[:, tile:] = dup_low
    total[...] += dot_right_t(both[...], weights[...])

    @pl.when(step == pl.num_programs(0) - 1)
    def _():
        dinputs[...] = total[...].astype(LOW)
        for copy in copies:
            copy.wait()


def feed_tile(units):
    return 256 if units % 256 == 0 else units


def by_tiles(gate, up):
    rows, units = gate.shape
    tile = feed_tile(units)

    def kernel(gate_ref, up_ref, out):
        for at in range(0, units, tile):
            out[:, 2 * at : 2 * at + tile] = gate_ref[:, at : at + tile]
            out[:, 2 * at + tile : 2 * at + 2 * tile] = up_ref[:, at : at + tile]

    return pl.pallas_call(
        kernel,
        out_shape=jax.ShapeDtypeStruct((rows, 2 * units), gate.dtype),
        compiler_params=params(),
        cost_estimate=cost(0, 8 * rows * units),
    )(gate, up)


def feed(ids, hidden, attn, gain, gate_up, dproduct):
    rows, width = hidden.shape
    units = dproduct.shape[1]
    tile = feed_tile(units)
    tspec = pl.BlockSpec((rows, tile), lambda step, *_: (0, step))
    anywhere = pl.BlockSpec(memory_space=pl.ANY)
    return pl.pallas_call(
        feed_kernel,
        grid_spec=pltpu.PrefetchScalarGridSpec(
            num_scalar_prefetch=1,
            grid=(units // tile,),
            in_specs=[whole((rows, width)), whole((rows, width)), whole(gain.shape)]
            + [pl.BlockSpec((width, 2 * tile), lambda step, *_: (0, step)), tspec],
            out_specs=[tspec, tspec, tspec, whole((rows, width)), anywhere, anywhere],
            scratch_shapes=[
                pltpu.VMEM((rows, width), F32),
                pltpu.VMEM((rows, 2 * tile), LOW),
                pltpu.VMEM((rows, width), F32),
                pltpu.VMEM((rows, width), LOW),
                pltpu.SemaphoreType.DMA((2,)),
            ],
        ),
        out_shape=[jax.ShapeDtypeStruct((rows, units), LOW)] * 3
        + [jax.ShapeDtypeStruct((rows, width), kind) for kind in (LOW, F32, LOW)],
        compiler_params=params(),
        cost_estimate=cost(8 * rows * width * units, 4 * width * units + 10 * rows * units),
    )(ids, hidden, attn, gain, gate_up, dproduct)


def shards(
    hidden_in,
    segments,
    cotangent,
    attn_gain,
    query_weight,
    key_weight,
    value_weight,
    output_weight,
    qnorm_gain,
    knorm_gain,
    ffn_gain,
    gate_weight,
    up_weight,
    down_weight,
):
    is_staged = lax.axis_size("fsdp") == 2 and lax.axis_size("context") == 4
    gather_fast = staged_gather if is_staged else gather_rows
    scatter_fast = staged_scatter if is_staged else scatter_rows
    head_dim = qnorm_gain.shape[0]
    local_rows, width = hidden_in.shape
    shard_rows = query_weight.shape[0]
    pieces = lax.axis_size("context")
    total_rows = local_rows * pieces
    half_rows = local_rows // 2
    value_heads = key_weight.shape[1] // head_dim
    qcols = query_weight.shape[1]
    kcols = key_weight.shape[1]

    def unmixed(both, which):
        starts = [(2 * head + which) * head_dim for head in range(value_heads)]
        return jnp.concatenate([both[:, at : at + head_dim] for at in starts], axis=1)

    blocks = staged_blocks() if is_staged else jnp.zeros((1,), jnp.int32)
    count = blocks.shape[0]
    near_shard = assemble(key_weight, value_weight, query_weight, head_dim)
    gain_shard, near_shard = tie(jnp.stack([attn_gain, ffn_gain]), near_shard)
    gains = staged_direct(gain_shard) if is_staged else gather_rows(gain_shard)
    gains = gains.reshape(-1, 2, shard_rows).astype(F32)
    gain_one = gains[:, 0].reshape(count, -1)
    gain_two = gains[:, 1].reshape(count, -1)

    me = lax.axis_index("context")
    last = 2 * pieces - 1
    spots = []
    for block in range(2 * pieces):
        owner = block if block < pieces else last - block
        spots.append(2 * (owner ^ me) + (0 if block < pieces else 1))
    info = jnp.stack([me, last - me] + spots).astype(jnp.int32)
    ramp = jnp.arange(half_rows, dtype=jnp.int32)
    positions = jnp.concatenate([me * half_rows + ramp, (last - me) * half_rows + ramp])
    seg_col = jnp.concatenate(
        [
            lax.dynamic_slice_in_dim(segments[0], block * half_rows, half_rows)
            for block in (me, last - me)
        ]
    )[:, None]
    seg_col = jnp.broadcast_to(seg_col, (local_rows, head_dim))
    half_dim = head_dim // 2
    inverse = THETA ** (-(jnp.arange(half_dim).astype(F32) * 2.0 / head_dim))
    angles = positions.astype(F32)[:, None] * inverse[None, :]
    cosine = jnp.cos(angles)
    sine = jnp.sin(angles)
    cosine = jnp.concatenate([cosine, cosine], axis=1)
    sine = jnp.concatenate([-sine, sine], axis=1)
    qgain = qnorm_gain.astype(F32)[None, :]
    kgain = knorm_gain.astype(F32)[None, :]

    (cot_staged,) = row_call(stage_kernel, blocks, [cotangent], [LOW])
    out_blocks = staged_blocks("y") if is_staged else blocks
    if is_staged:
        match = (out_blocks[:, None] == blocks[None, :]).astype(F32)
        gain_two = jnp.dot(match, gain_two, precision=lax.Precision.HIGHEST)
    if is_staged:
        near_first = staged(near_shard, "xy")
        near_second = staged(near_shard, "yx")
        near_both, gain_one = tie(staged(near_first, "yx"), gain_one)
        near_parts = [near_shard, near_first, near_second, near_both]
        near_last, out_shard = tie(staged(near_both, "core"), output_weight)
        near_halves = near_parts + [staged(part, "core") for part in near_parts[:3]] + [near_last]
        out_pair = staged_pair(out_shard, "y")
    else:
        near_halves = [gather_rows(near_shard)]
    (inputs_one,) = row_call(first_norm_kernel, blocks, [hidden_in], [LOW], gain_one, [info, seg_col, cosine, sine, qgain, kgain, gain_two], mib=20)
    kv_proj, query_proj, kv_own = opening(inputs_one, near_halves, 2 * kcols, qcols, kgain, cosine, sine)
    if is_staged:
        out_pair, kv_own = tie(out_pair, kv_own)
        out_halves = staged_halves(staged_quad(out_pair, "y"))
    else:
        out_halves = [gather_rows(output_weight)]
    kv_across = swap_context(kv_own, 2)
    kv_pieces = [kv_own, swap_context(kv_own, 1), kv_across, swap_context(kv_across, 1)]
    gate_up_shard, kv_proj = tie(by_tiles(gate_weight, up_weight), kv_proj)
    gate_up = gather_rows(gate_up_shard)
    attended, attended_wide, logs, attn_part = attend(
        info, query_proj, out_halves, kv_pieces, qgain, cosine, sine, segments, seg_col
    )
    down_shard, logs = tie(down_weight, logs)
    down_full = gather_fast(down_shard)
    attn_out = sum_tensor(attn_part)
    dproduct = dot_plain(cot_staged, down_full)
    near_full = jnp.concatenate(near_halves)
    out_full = jnp.concatenate(out_halves)
    attn_out, dproduct, near_full, out_full = tie(attn_out, dproduct, near_full, out_full)
    product, dgate, dup_low, dnormed_two_part, middle, inputs_two = feed(
        out_blocks, hidden_in, attn_out, gain_two, gate_up, dproduct
    )
    dnormed_two = sum_tensor(dnormed_two_part)

    ffn_part = dot_right_t(product, down_full).astype(LOW)
    down_own = scatter_rows(dot_left_t(cotangent, product))
    grad_gate = dot_left_t(inputs_two, dgate).astype(LOW)
    grad_up = dot_left_t(inputs_two, dup_low).astype(LOW)
    dnormed_two, ffn_part, grad_gate, grad_up = tie(dnormed_two, ffn_part, grad_gate, grad_up)
    ffn_out = sum_tensor(ffn_part)
    dmiddle, dattn, gain_two_sums = row_call(
        second_back_kernel, out_blocks, [dnormed_two, middle, cotangent], [LOW, LOW], gain_two, sums=True
    )
    gain_two_part = jnp.sum(gain_two_sums, axis=0) / lax.axis_size("tensor")
    dattended = dot_plain(dattn, out_full).astype(LOW)
    dquery, dkv_keep, dkv_send, qnorm_parts = attend_back(
        info, query_proj, attended_wide, logs, dattended, kv_pieces, qgain, cosine, sine, segments, seg_col
    )
    grad_gate, down_own, qnorm_parts = tie(grad_gate, down_own, qnorm_parts)
    gate_own = scatter_rows(grad_gate)
    dkv_pair = add_low(dkv_keep, swap_context(dkv_send, 1))
    dkv, knorm_parts = key_backward(
        dkv_pair[:local_rows], swap_context(dkv_pair[local_rows:], 2), kv_proj, kgain, cosine, sine
    )
    grad_output = dot_left_t(dattn, attended).astype(LOW)
    output_own = staged_scatter(grad_output, "y") if is_staged else scatter_rows(grad_output)
    dqkv = jnp.concatenate([dkv, dquery], axis=1)
    dnormed_one_part = dot_right_t(dqkv, near_full).astype(LOW)
    later_part, ffn_out = tie(dnormed_one_part, ffn_out)
    dnormed_one = sum_tensor(later_part)
    grad_up, gate_own, ffn_out = tie(grad_up, gate_own, ffn_out)
    (output,) = row_call(output_kernel, blocks, [middle, ffn_out], [LOW])
    qkv_own = scatter_fast(dot_left_t(inputs_one, dqkv).astype(LOW))
    gain_one_part = jnp.sum(dnormed_one_part.astype(F32) * inputs_one.astype(F32), axis=0)
    up_own = scatter_rows(grad_up)
    if is_staged:
        onehot = (blocks[None, :] == jnp.arange(count, dtype=jnp.int32)[:, None]).astype(F32)
        gain_one_part = jnp.dot(
            onehot, gain_one_part.reshape(count, -1), precision=lax.Precision.HIGHEST
        ).reshape(-1)
    small = sum_all(
        jnp.concatenate(
            [gain_one_part, gain_two_part, jnp.sum(qnorm_parts, axis=(0, 1)), jnp.sum(knorm_parts, axis=0)]
        )
    )
    own = attn_gain.shape[0]
    start = lax.axis_index(ROWS) * own
    gain_one_grad = lax.dynamic_slice_in_dim(small[:width], start, own) / attn_gain.astype(F32)
    gain_two_grad = lax.dynamic_slice_in_dim(small[width : 2 * width], start, own)
    qnorm_total = small[2 * width : 2 * width + head_dim]
    knorm_total = small[2 * width + head_dim :]
    qkv_own = qkv_own.astype(F32)
    query_grad = qkv_own[:, 2 * kcols :]
    key_grad, value_grad = unmixed(qkv_own, 0), unmixed(qkv_own, 1)
    output_own = output_own.astype(F32)
    gate_own = gate_own.astype(F32)
    down_own = down_own.astype(F32)
    done = [output, small, query_grad, key_grad, value_grad, output_own, gate_own, down_own]
    (input_grad,) = row_call(
        first_back_kernel, blocks, [dnormed_one, hidden_in, dmiddle], [F32], gain_one, after=done
    )
    return (
        output,
        input_grad,
        gain_one_grad,
        query_grad,
        key_grad,
        value_grad,
        output_own,
        qnorm_total,
        knorm_total,
        gain_two_grad,
        gate_own,
        up_own.astype(F32),
        down_own,
    )


def solution(mesh):
    in_specs = (
        P(("fsdp", "context"), None),
        P("fsdp", None),
        P(("fsdp", "context"), None),
        P(("fsdp", "context")),
        P(("fsdp", "context"), "tensor"),
        P(("fsdp", "context"), "tensor"),
        P(("fsdp", "context"), "tensor"),
        P(("fsdp", "context"), "tensor"),
        P(),
        P(),
        P(("fsdp", "context")),
        P(("fsdp", "context"), "tensor"),
        P(("fsdp", "context"), "tensor"),
        P(("fsdp", "context"), "tensor"),
    )
    out_specs = (
        P(("fsdp", "context"), None),
        P(("fsdp", "context"), None),
        P(("fsdp", "context")),
        P(("fsdp", "context"), "tensor"),
        P(("fsdp", "context"), "tensor"),
        P(("fsdp", "context"), "tensor"),
        P(("fsdp", "context"), "tensor"),
        P(),
        P(),
        P(("fsdp", "context")),
        P(("fsdp", "context"), "tensor"),
        P(("fsdp", "context"), "tensor"),
        P(("fsdp", "context"), "tensor"),
    )
    return jax.shard_map(shards, mesh=mesh, in_specs=in_specs, out_specs=out_specs, check_vma=False)
```
